256 devices in a mesh: dp: 64 (over x, z, core), proto: 4 (over y).
Axes of the slice: x: 4, y: 4, z: 8, core: 2. Of those that a mesh axis runs over, the one named last changes fastest.
Arguments:
- embeddings: bfloat16 [32768, 256], P('dp'), may hold values from -1.5 to 1.5
- prototypes: bfloat16 [16384, 256], P('proto'), may hold values from -0.35 to 0.35
- pair_index: int32 [32768], P('dp'), may hold values from 0 to 511, as said below
Outputs:
- grad_embeddings: float32 [32768, 256], P('dp')
- grad_prototypes: float32 [16384, 256], P(('proto', 'dp'))
The draws below stay inside these ranges and needn't reach their ends.
Inputs may be any that keep to these rules, and one draw needn't show every extreme that they name: Within each aligned block of 512 rows the rows are paired off: pair_index maps each row to its partner, partner of partner is the row itself, and no row is its own partner.
All inputs are finite; a program needn't handle non-finite values.
Results may differ from the reference program's by a relative error of at most 0.0033.
Values may be sent and summed in bfloat16 or wider, within the bound.
A program may use at most 128 MiB of HBM per device.

```python
import jax
import jax.numpy as jnp
import numpy as np
from jax import lax

D = 256
K = 16384
ITERS = 3
B_DEV = 512
TOKENS = 32768


cluster_bounds = np.array([368, 552, 675, 767, 841, 902, 954], dtype=np.int32)


cluster_total = 8


def shared_centers(key):
    return jnp.clip(jax.random.normal(key, (cluster_total, D), jnp.float32), -4.0, 4.0)


def cluster_label(samples):
    bounds = jnp.asarray(cluster_bounds)
    return jnp.sum((samples[:, None] >= bounds[None, :]).astype(jnp.int32), axis=1).astype(jnp.int32)


def pair_block(key):
    order = jax.random.permutation(key, B_DEV).astype(jnp.int32)
    first = order[0::2]
    second = order[1::2]
    result = jnp.zeros((B_DEV,), jnp.int32)
    result = result.at[first].set(second)
    return result.at[second].set(first)


def draw_pair_index(key, part):
    key = jax.random.fold_in(key, 7)
    keys = jax.random.split(key, TOKENS // B_DEV)
    return jax.vmap(pair_block)(keys).reshape(TOKENS).astype(jnp.int32)


def draw_embeddings(key, part):
    centers = shared_centers(key)
    key = jax.random.fold_in(key, 11)
    keys = jax.random.split(key, 5)
    blocks = TOKENS // B_DEV
    block_ids = jnp.arange(TOKENS, dtype=jnp.int32) // B_DEV
    position = ((2 * block_ids + 1) * 1000 // (2 * blocks)).astype(jnp.int32)
    order = jax.random.permutation(keys[0], cluster_total).astype(jnp.int32)
    dominant = order[cluster_label(position)]
    others = order[cluster_label(jax.random.randint(keys[1], (TOKENS,), 0, 1000).astype(jnp.int32))]
    picked = jax.random.randint(keys[2], (TOKENS,), 0, 10) < 6
    labels = jnp.where(picked, dominant, others)
    noise = jnp.clip(jax.random.normal(keys[3], (TOKENS, D), jnp.float32), -4.0, 4.0)
    scales = jnp.exp(jax.random.uniform(keys[4], (TOKENS, 1), jnp.float32, -0.69, 0.69))
    mixed = 0.5 * centers[labels] + 0.866 * noise
    return (scales * mixed / 8.0).astype(jnp.bfloat16)


def draw_prototypes(key, part):
    centers = shared_centers(key)
    key = jax.random.fold_in(key, 13)
    keys = jax.random.split(key, 4)
    index = jnp.arange(K, dtype=jnp.int32)
    placed = jax.random.permutation(keys[2], cluster_total).astype(jnp.int32)
    local_group = placed[index * cluster_total // K]
    random_group = jax.random.randint(keys[0], (K,), 0, cluster_total).astype(jnp.int32)
    take_local = jax.random.randint(keys[3], (K,), 0, 10) < 7
    groups = jnp.where(take_local, local_group, random_group)
    position = (index.astype(jnp.float32) + 0.5) / K
    weight = 0.3 + 0.3 * position
    rest = jnp.sqrt(1.0 - weight * weight)
    noise = jnp.clip(jax.random.normal(keys[1], (K, D), jnp.float32), -4.0, 4.0)
    mixed = weight[:, None] * centers[groups] + rest[:, None] * noise
    return (mixed / 16.0).astype(jnp.bfloat16)


def setup_inputs(seed: int = 0) -> dict:
    seeds = jax.random.split(jax.random.key(seed), 4)
    return {
        "embeddings": draw_embeddings(jax.random.fold_in(seeds[3], 71), 0),
        "prototypes": draw_prototypes(jax.random.fold_in(seeds[3], 71), 0),
        "pair_index": draw_pair_index(jax.random.fold_in(seeds[3], 71), 0),
    }


sink_eps = 0.05
sharpness_divisor = 0.1
objective_factor = 1.0

def unit_rows(matrix):
    values = matrix.astype(jnp.float32)
    norms = jnp.sqrt(lax.optimization_barrier(jnp.sum(values * values, axis=1, keepdims=True)) + 1e-06)
    return (values / norms, norms)

def reference(embeddings, prototypes, pair_index):
    unit_z, norm_z = unit_rows(embeddings)
    unit_c, norm_c = unit_rows(prototypes)
    z_hat = unit_z.astype(jnp.bfloat16)
    c_hat = unit_c.astype(jnp.bfloat16)
    blocks = TOKENS // B_DEV
    z_blocks = z_hat.astype(jnp.float32).reshape(blocks, B_DEV, D)
    c_full = c_hat.astype(jnp.float32)
    hp = lax.Precision.HIGHEST

    def scores_of(block):
        return jnp.dot(block, c_full.T, precision=hp)
    row_scale = jnp.ones((blocks, B_DEV), jnp.float32)
    col_scale = jnp.ones((K,), jnp.float32)
    for step in range(ITERS):

        def column_pass(total, item):
            block, rows = item
            kernel = jnp.exp(scores_of(block) / sink_eps)
            return (total + jnp.dot(rows, kernel, precision=hp), None)
        totals, _ = lax.scan(column_pass, jnp.zeros((K,), jnp.float32), (z_blocks, row_scale))
        col_scale = 1.0 / totals

        def row_pass(block):
            kernel = jnp.exp(scores_of(block) / sink_eps)
            return jnp.dot(kernel, col_scale, precision=hp)
        row_scale = 1.0 / lax.map(row_pass, z_blocks)
    pairs = pair_index.reshape(blocks, B_DEV).astype(jnp.int32)

    def backward(total, item):
        block, rows, partner = item
        cluster_affinity = scores_of(block)
        kernel = jnp.exp(cluster_affinity / sink_eps)
        raised_power = jnp.exp(cluster_affinity / sharpness_divisor)
        predicted_likelihood = raised_power / lax.optimization_barrier(jnp.sum(raised_power, axis=1, keepdims=True))
        codes = kernel * col_scale[None, :] * rows[:, None]
        crossed_assignment = jnp.take(codes, partner, axis=0)
        affinity_derivative = (objective_factor / sharpness_divisor * (predicted_likelihood - crossed_assignment)).astype(jnp.bfloat16)
        grad_f = affinity_derivative.astype(jnp.float32)
        grad_rows = jnp.dot(grad_f, c_full, precision=hp)
        total = total + jnp.dot(grad_f.T, block, precision=hp)
        return (total, grad_rows)
    grad_chat, grad_zhat = lax.scan(backward, jnp.zeros((K, D), jnp.float32), (z_blocks, row_scale, pairs))
    grad_zhat = grad_zhat.reshape(TOKENS, D)
    grad_embeddings = (grad_zhat - unit_z * lax.optimization_barrier(jnp.sum(unit_z * grad_zhat, axis=1, keepdims=True))) / norm_z
    grad_prototypes = (grad_chat - unit_c * lax.optimization_barrier(jnp.sum(unit_c * grad_chat, axis=1, keepdims=True))) / norm_c
    return (grad_embeddings, grad_prototypes)
```

```python
import jax
import jax.numpy as jnp
from jax import lax
from jax.experimental import pallas as pl
from jax.experimental.pallas import tpu as pltpu
from jax.sharding import PartitionSpec as P

X, Z, C, Y = 4, 8, 2, 4
MESH = pl.DeviceIdType.MESH
F32, BF16 = jnp.float32, jnp.bfloat16
NT = (((1,), (1,)), ((), ()))
NN = (((1,), (0,)), ((), ()))


def ring(k, n):
    return min(k, n - k)


def offsets(axes):
    span = [n if a in axes else 1 for a, n in zip("xzcy", (X, Z, C, Y))]
    out = [
        (a, b, e, f)
        for a in range(span[0])
        for b in range(span[1])
        for e in range(span[2])
        for f in range(span[3])
        if a or b or e or f
    ]
    out.sort(key=lambda t: -(4 * (ring(t[0], X) + ring(t[1], Z) + ring(t[3], Y)) + t[2]))
    return out


def dot(a, b, dims=NN):
    return lax.dot_general(a, b, dims, preferred_element_type=F32)


def unit(values):
    norm = jnp.sqrt(jnp.sum(values * values, axis=1, keepdims=True) + 1e-06)
    return values / norm, norm


def spread(row):
    return jnp.broadcast_to(row, (128, 128)).T


def make_kernel(B, D, NC):
    RT, RC, CC, TC = C * B, C * B // 128, NC // 128, NC // X
    OB = TC // Z
    BC = B // 128
    HB = B // 2
    XZ, YC, XYC = offsets("xz"), offsets("yc"), offsets("xyc")

    def kernel(
        emb_ref, proto_ref, pair_ref, gz_ref, gc_ref,
        praw, chat, ep, perm, permt, zall, E, K, ET, WT, G, GT, colacc, racc, rb, rpb, c3b,
        crow, rrow, rp4, r34, csend, crecv, rsend1, rrecv1, rsend2, rrecv2, rsend3, rrecv3,
        gpart, ksend, krecv, tpart, zsend, zrecv, ysend, yrecv, yall,
        lsem, core_s, core_r, xs, xr, fs, fr, cs, cr, rs, rr, ps, pr, ks, kr, zs, zr, ys, yr, gs, gr,
    ):
        dp = lax.axis_index("dp")
        iy = lax.axis_index("proto")
        ix, iz, ic = dp // (Z * C), (dp // C) % Z, dp % C

        def dev(o):
            a, b, e, f = o
            nx = (ix + a) % X if a else ix
            nz = (iz + b) % Z if b else iz
            nc = (ic + e) % C if e else ic
            ny = (iy + f) % Y if f else iy
            return {"dp": (nx * Z + nz) * C + nc, "proto": ny}

        def send(src, dst, s, r, o):
            pltpu.make_async_remote_copy(
                src_ref=src, dst_ref=dst, send_sem=s, recv_sem=r, device_id=dev(o), device_id_type=MESH
            ).start()

        def take(ref, sem):
            pltpu.make_async_copy(ref, ref, sem).wait()

        load = pltpu.make_async_copy(proto_ref.at[:, ic], praw, lsem.at[0])
        load.start()
        barrier = pltpu.get_barrier_semaphore()
        everyone = sorted(set(XZ + YC + XYC))
        for o in everyone:
            pl.semaphore_signal(barrier, inc=1, device_id=dev(o), device_id_type=MESH)

        pair = pair_ref[...]
        lane = lax.broadcasted_iota(jnp.int32, (1, B), 1)
        first = (lane < pair).astype(F32)
        up = (
            lax.broadcasted_iota(jnp.int32, (B, B), 0) < lax.broadcasted_iota(jnp.int32, (B, B), 1)
        ).astype(F32).astype(BF16)
        rank = dot(jnp.broadcast_to(first, (8, B)).astype(BF16), up)[0:1, :]
        slot = jnp.where(first > 0.5, rank, -1.0).astype(jnp.int32)
        top = (lax.broadcasted_iota(jnp.int32, (HB, B), 0) == slot).astype(F32).astype(BF16)
        partner = (lax.broadcasted_iota(jnp.int32, (B, B), 0) == pair).astype(F32).astype(BF16)
        perm[0:HB, :] = top
        perm[HB:B, :] = dot(top, partner).astype(BF16)
        ep[...] = dot(perm[...], emb_ref[...]).astype(BF16)
        uz, _ = unit(ep[...].astype(F32))
        zall[ix, ic] = uz.astype(BF16)

        load.wait()

        def norm_c(i, _):
            uc, _n = unit(praw[i].astype(F32))
            chat[pl.ds(pl.multiple_of(i * OB, OB), OB), :] = uc.astype(BF16)
            return 0

        lax.fori_loop(0, X * Z, norm_c, 0)

        def scores(h, fresh):
            rows = pl.ds(pl.multiple_of(h * B, B), B)
            zb = zall[ix, h]
            racc[rows, :] = jnp.zeros((B, 128), F32)

            def step(j, _):
                cols = pl.ds(pl.multiple_of(j * 256, 256), 256)
                e = jnp.exp(dot(zb, chat[cols, :], NT) * 10.0)
                E[rows, cols] = e
                k = e * e
                K[rows, cols] = k
                part = jnp.sum(k.reshape(B // 8, 8, 256), axis=0)
                colacc[:, cols] = part if fresh else colacc[:, cols] + part
                racc[rows, :] = racc[rows, :] + (e[:, :128] + e[:, 128:])
                return 0

            lax.fori_loop(0, NC // 256, step, 0)

        scores(ic, True)
        pl.semaphore_wait(barrier, len(everyone))
        send(zall.at[ix, ic], zall.at[ix, ic], core_s, core_r, (0, 0, 1, 0))
        take(zall.at[ix, 1 - ic], core_r)
        scores(1 - ic, False)

        def col_send(t):
            for j in range(CC):
                crow[j : j + 1, :] = jnp.sum(colacc[:, j * 128 : (j + 1) * 128], axis=0, keepdims=True)
            csend[t] = crow[...].astype(BF16)
            for i, o in enumerate(XZ):
                send(csend.at[t], crecv.at[t, i + 1], cs.at[t], cr.at[t], o)
            pltpu.make_async_copy(csend.at[t], crecv.at[t, 0], cr.at[t]).start()

        def col_take(t):
            take(crecv.at[t], cr.at[t])
            crow[...] = 1.0 / jnp.sum(crecv[t].astype(F32), axis=0)

        def row_pass(out, keep):
            def step(i, _):
                rows = pl.ds(pl.multiple_of(i * 128, 128), 128)
                acc = jnp.zeros((128, 128), F32)
                for j in range(CC):
                    w = K[rows, j * 128 : (j + 1) * 128] * crow[j : j + 1, :]
                    if keep:
                        K[rows, j * 128 : (j + 1) * 128] = w
                    acc = acc + w
                out[pl.ds(i, 1), :] = jnp.sum(acc.T, axis=0, keepdims=True)
                return 0

            lax.fori_loop(0, RC, step, 0)

        def col_pass():
            colacc[...] = jnp.zeros((8, NC), F32)

            def step(i, _):
                rows = pl.ds(pl.multiple_of(i * 128, 128), 128)
                r = rb[rows, :]
                for j in range(CC):
                    cols = slice(j * 128, (j + 1) * 128)
                    p = K[rows, cols] * r
                    colacc[:, cols] = colacc[:, cols] + jnp.sum(p.reshape(16, 8, 128), axis=0)
                return 0

            lax.fori_loop(0, RC, step, 0)

        def scores_t(lo, hi):
            def step(n, _):
                x, c, q = n // (C * B // 256), (n // (B // 256)) % C, n % (B // 256)
                zb = zall[x, c, pl.ds(pl.multiple_of(q * 256, 256), 256), :]
                mine = chat[pl.ds(pl.multiple_of(ix * TC, TC), TC), :]
                ET[:, pl.ds(pl.multiple_of(n * 256, 256), 256)] = jnp.exp(dot(mine, zb, NT) * 10.0)
                return 0

            lax.fori_loop(lo, hi, step, 0)

        col_send(0)
        for a in range(1, X):
            send(zall.at[ix, ic], zall.at[ix, ic], xs, xr.at[a], (a, 0, 0, 0))
        for i in range(RC):
            rsend1[RC + i : RC + i + 1, :] = jnp.sum(racc[i * 128 : (i + 1) * 128, :].T, axis=0, keepdims=True)
        permt[...] = perm[...].astype(F32).T.astype(BF16)
        col_take(0)
        row_pass(rsend1, False)
        for i, o in enumerate(YC):
            send(rsend1, rrecv1.at[i + 1], rs.at[0], rr.at[0], o)
        pltpu.make_async_copy(rsend1, rrecv1.at[0], rr.at[0]).start()
        take(rrecv1, rr.at[0])
        totals = jnp.sum(rrecv1[...], axis=0)
        rrow[...] = 1.0 / totals[:RC, :]
        rp4[ix] = 10.0 / totals[RC:, :]

        for i in range(RC):
            rb[i * 128 : (i + 1) * 128, :] = spread(rrow[i : i + 1, :])
        col_pass()
        col_send(1)
        for a in range(1, X):
            send(rp4.at[ix], rp4.at[ix], ps, pr.at[a], (a, 0, 0, 0))
        for a in range(1, X):
            src = (ix + X - a) % X
            take(zall.at[src, ic], xr.at[a])
            send(zall.at[src, ic], zall.at[src, ic], fs, fr.at[a], (0, 0, 1, 0))
        for i in range(RC):
            rpb[i * 128 : (i + 1) * 128, :] = spread(rp4[ix, i : i + 1, :])
        col_take(1)
        row_pass(rsend2, False)
        for i, o in enumerate(YC):
            send(rsend2, rrecv2.at[i + 1], rs.at[1], rr.at[1], o)
        pltpu.make_async_copy(rsend2, rrecv2.at[0], rr.at[1]).start()
        for a in range(1, X):
            take(zall.at[(ix + X - a) % X, 1 - ic], fr.at[a])
        NB = X * C * B // 256
        scores_t(0, NB // 2)
        take(rrecv2, rr.at[1])
        rrow[...] = 1.0 / jnp.sum(rrecv2[...], axis=0)

        for i in range(RC):
            rb[i * 128 : (i + 1) * 128, :] = spread(rrow[i : i + 1, :])
        col_pass()
        col_send(2)
        scores_t(NB // 2, NB)
        for a in range(1, X):
            take(rp4.at[(ix + X - a) % X], pr.at[a])
        col_take(2)
        row_pass(rsend3, True)
        YCI = {o: i + 1 for i, o in enumerate(YC)}
        YCI[(0, 0, 0, 0)] = 0
        for o in XYC:
            send(rsend3, rrecv3.at[ix * (len(YC) + 1) + YCI[(0,) + o[1:]]], rs.at[2], rr.at[2], o)
        pltpu.make_async_copy(rsend3, rrecv3.at[ix * (len(YC) + 1)], rr.at[2]).start()
        mine = crow[pl.ds(ix * (TC // 128), TC // 128), :]
        for i in range(TC // 128):
            c3b[i * 128 : (i + 1) * 128, :] = spread(mine[i : i + 1, :])

        def weigh(n, _):
            x = n // RC
            q = n % RC
            cols = pl.ds(pl.multiple_of(n * 128, 128), 128)
            e = ET[:, cols]
            WT[:, cols] = e * e * c3b[...]
            ET[:, cols] = e * rp4[x, pl.ds(q, 1), :]
            return 0

        lax.fori_loop(0, X * RC, weigh, 0)
        take(rrecv3, rr.at[2])
        for x in range(X):
            r34[x] = 10.0 / jnp.sum(rrecv3[x * (len(YC) + 1) : (x + 1) * (len(YC) + 1)], axis=0)
        for i in range(RC):
            rb[i * 128 : (i + 1) * 128, :] = spread(r34[ix, pl.ds(i, 1), :])

        def grad_r(i, _):
            ip = (i // BC) * BC + (i + BC // 2) % BC
            rows = pl.ds(pl.multiple_of(i * 128, 128), 128)
            prows = pl.ds(pl.multiple_of(ip * 128, 128), 128)
            rp, r3 = rpb[rows, :], rb[prows, :]
            for j in range(CC):
                cols = slice(j * 128, (j + 1) * 128)
                G[rows, cols] = (E[rows, cols] * rp - K[prows, cols] * r3).astype(BF16)
            return 0

        lax.fori_loop(0, RC, grad_r, 0)

        def mm_r(i, _):
            rows = pl.ds(pl.multiple_of(i * 256, 256), 256)
            gpart[rows, :] = dot(G[rows, :], chat[...])
            return 0

        lax.fori_loop(0, RT // 256, mm_r, 0)
        mine_rows = pl.ds(pl.multiple_of(ic * B, B), B)
        other_rows = pl.ds(pl.multiple_of((1 - ic) * B, B), B)
        ksend[...] = gpart[other_rows, :].astype(BF16)
        send(ksend, krecv, ks, kr, (0, 0, 1, 0))

        def grad_t(n, _):
            x, q = n // RC, n % RC
            qp = (q // BC) * BC + (q + BC // 2) % BC
            cols = pl.ds(pl.multiple_of(n * 128, 128), 128)
            pcols = pl.ds(pl.multiple_of((x * RC + qp) * 128, 128), 128)
            GT[:, cols] = (ET[:, cols] - WT[:, pcols] * r34[x, pl.ds(qp, 1), :]).astype(BF16)
            return 0

        lax.fori_loop(0, X * RC, grad_t, 0)
        zflat = zall[...].reshape(X * RT, D)

        def mm_t(i, _):
            rows = pl.ds(pl.multiple_of(i * 256, 256), 256)
            tpart[rows, :] = dot(GT[rows, :], zflat)
            return 0

        lax.fori_loop(0, TC // 256, mm_t, 0)
        zsend[...] = tpart[...].reshape(Z, OB, D).astype(BF16)
        for b in sorted(range(1, Z), key=lambda k: -ring(k, Z)):
            send(zsend.at[(iz + b) % Z], zrecv.at[b - 1], zs, zr, (0, b, 0, 0))

        take(krecv, kr)
        gpart[mine_rows, :] = gpart[mine_rows, :] + krecv[...].astype(F32)
        ysend[...] = gpart[mine_rows, :].reshape(Y, B // Y, D).astype(BF16)
        for f in sorted(range(1, Y), key=lambda k: -ring(k, Y)):
            send(ysend.at[(iy + f) % Y], yrecv.at[f - 1], ys, yr, (0, 0, 0, f))

        take(zrecv, zr)
        gcs = tpart[pl.ds(pl.multiple_of(iz * OB, OB), OB), :]
        gcs = gcs + jnp.sum(zrecv[...].astype(F32), axis=0)
        uc, nc = unit(praw[ix * Z + iz].astype(F32))
        gc_ref[...] = (gcs - uc * jnp.sum(uc * gcs, axis=1, keepdims=True)) / nc

        take(yrecv, yr)
        QB = B // Y
        gzs = gpart[pl.ds(pl.multiple_of(ic * B + iy * QB, QB), QB), :]
        gzs = gzs + jnp.sum(yrecv[...].astype(F32), axis=0)
        uq, nq = unit(ep[pl.ds(pl.multiple_of(iy * QB, QB), QB), :].astype(F32))
        yall[iy] = ((gzs - uq * jnp.sum(uq * gzs, axis=1, keepdims=True)) / nq).astype(BF16)
        for f in sorted(range(1, Y), key=lambda k: -ring(k, Y)):
            send(yall.at[iy], yall.at[iy], gs, gr, (0, 0, 0, f))
        take(yall.at[pl.ds(0, Y - 1)], gr)
        gz_ref[...] = dot(permt[...], yall[...].reshape(B, D))

        take(zall.at[ix, ic], core_s)
        take(zall.at[pl.ds(0, X - 1), 0], xs)
        take(zall.at[pl.ds(0, X - 1), 0], fs)
        take(rp4.at[pl.ds(0, X - 1)], ps)
        for t in range(3):
            take(crecv.at[t, pl.ds(0, len(XZ))], cs.at[t])
        take(rrecv1.at[pl.ds(0, len(YC))], rs.at[0])
        take(rrecv2.at[pl.ds(0, len(YC))], rs.at[1])
        take(rrecv3.at[pl.ds(0, len(XYC))], rs.at[2])
        take(ksend, ks)
        take(zrecv, zs)
        take(yrecv, ys)
        take(yall.at[pl.ds(0, Y - 1)], gs)

    V = pltpu.VMEM
    S = pltpu.SemaphoreType.DMA
    QB = B // Y
    scratch = [
        V((X * Z, OB, D), BF16),
        V((NC, D), BF16),
        V((B, D), BF16),
        V((B, B), BF16),
        V((B, B), BF16),
        V((X, C, B, D), BF16),
        V((RT, NC), F32),
        V((RT, NC), F32),
        V((TC, X * RT), F32),
        V((TC, X * RT), F32),
        V((RT, NC), BF16),
        V((TC, X * RT), BF16),
        V((8, NC), F32),
        V((RT, 128), F32),
        V((RT, 128), F32),
        V((RT, 128), F32),
        V((TC, 128), F32),
        V((CC, 128), F32),
        V((RC, 128), F32),
        V((X, RC, 128), F32),
        V((X, RC, 128), F32),
        V((3, CC, 128), BF16),
        V((3, len(XZ) + 1, CC, 128), BF16),
        V((2 * RC, 128), F32),
        V((len(YC) + 1, 2 * RC, 128), F32),
        V((RC, 128), F32),
        V((len(YC) + 1, RC, 128), F32),
        V((RC, 128), F32),
        V((X * (len(YC) + 1), RC, 128), F32),
        V((RT, D), F32),
        V((B, D), BF16),
        V((B, D), BF16),
        V((TC, D), F32),
        V((Z, OB, D), BF16),
        V((Z - 1, OB, D), BF16),
        V((Y, QB, D), BF16),
        V((Y - 1, QB, D), BF16),
        V((Y, QB, D), BF16),
        S((1,)),
        S, S,
        S, S((X,)),
        S, S((X,)),
        S((3,)), S((3,)),
        S((3,)), S((3,)),
        S, S((X,)),
        S, S,
        S, S,
        S, S,
        S, S,
    ]
    return kernel, scratch


def body(embeddings, prototypes, pair_index):
    B, D = embeddings.shape
    NCL = prototypes.shape[0]
    NC = NCL // C
    OB = NCL // (X * Z * C)
    kernel, scratch = make_kernel(B, D, NC)
    vm = pl.BlockSpec(memory_space=pltpu.VMEM)
    return pl.pallas_call(
        kernel,
        out_shape=(jax.ShapeDtypeStruct((B, D), F32), jax.ShapeDtypeStruct((OB, D), F32)),
        in_specs=[vm, pl.BlockSpec(memory_space=pl.ANY), vm],
        out_specs=(vm, vm),
        scratch_shapes=scratch,
        compiler_params=pltpu.CompilerParams(
            collective_id=0, has_side_effects=True, vmem_limit_bytes=60 * 2**20
        ),
        name="swav",
    )(embeddings, prototypes.reshape(X * Z, C, OB, D), pair_index.reshape(1, B))


def solution(mesh):
    return jax.shard_map(
        body,
        mesh=mesh,
        in_specs=(P("dp", None), P("proto", None), P("dp")),
        out_specs=(P("dp", None), P(("proto", "dp"), None)),
        check_vma=False,
    )
```

```python
import jax
import jax.numpy as jnp
from jax import lax
from jax.experimental import pallas as pl
from jax.experimental.pallas import tpu as pltpu
from jax.sharding import PartitionSpec as P

X, Z, C, Y = 4, 8, 2, 4
MESH = pl.DeviceIdType.MESH
F32, BF16 = jnp.float32, jnp.bfloat16
NT = (((1,), (1,)), ((), ()))
NN = (((1,), (0,)), ((), ()))


def ring(k, n):
    return min(k, n - k)


def offsets(axes):
    span = [n if a in axes else 1 for a, n in zip("xzcy", (X, Z, C, Y))]
    out = [
        (a, b, e, f)
        for a in range(span[0])
        for b in range(span[1])
        for e in range(span[2])
        for f in range(span[3])
        if a or b or e or f
    ]
    out.sort(key=lambda t: -(4 * (ring(t[0], X) + ring(t[1], Z) + ring(t[3], Y)) + t[2]))
    return out


def dot(a, b, dims=NN):
    return lax.dot_general(a, b, dims, preferred_element_type=F32)


def unit(values):
    norm = jnp.sqrt(jnp.sum(values * values, axis=1, keepdims=True) + 1e-06)
    return values / norm, norm


def spread(row):
    return jnp.broadcast_to(row, (128, 128)).T


def make_kernel(B, D, NC):
    RT, RC, CC, TC = C * B, C * B // 128, NC // 128, NC // X
    OB = TC // Z
    BC = B // 128
    HB = B // 2
    FZ = sorted(range(Z), key=lambda k: -ring(k, Z))
    NEAR, FAR = (1, X - 1), 2
    XZ, YC, XYC = offsets("xz"), offsets("yc"), offsets("xyc")

    GR = len(YC) + 1
    YCI = {o: i + 1 for i, o in enumerate(YC)}
    YCI[(0, 0, 0, 0)] = 0

    def kernel(
        emb_ref, proto_ref, pair_ref, gz_ref, gc_ref,
        pair_v, emb_v, praw, chat, ep, perm, permt, zall, E, K, ET, WT, colacc, racc, rb, rpb, c3a, c3b, mine_c,
        crow, rrow, rp4, r34, csend, crecv, rsend1, rrecv1, rsend2, rrecv2, rsend3, rrecv3,
        gpart, ksend, krecv, tpart, zsend, zrecv, ysend, yrecv, yall,
        lsem, core_s, core_r, xs, xr, fs, fr, cs, cr, rs, rr, ps, pr, ks, kr, zs, zr, ys, yr, gs, gr,
    ):
        dp = lax.axis_index("dp")
        iy = lax.axis_index("proto")
        ix, iz, ic = dp // (Z * C), (dp // C) % Z, dp % C

        def dev(o):
            a, b, e, f = o
            nx = (ix + a) % X if a else ix
            nz = (iz + b) % Z if b else iz
            nc = (ic + e) % C if e else ic
            ny = (iy + f) % Y if f else iy
            return {"dp": (nx * Z + nz) * C + nc, "proto": ny}

        def send(src, dst, s, r, o):
            pltpu.make_async_remote_copy(
                src_ref=src, dst_ref=dst, send_sem=s, recv_sem=r, device_id=dev(o), device_id_type=MESH
            ).start()

        def take(ref, sem):
            pltpu.make_async_copy(ref, ref, sem).wait()

        loads = [
            pltpu.make_async_copy(pair_ref, pair_v, lsem.at[0]),
            pltpu.make_async_copy(emb_ref, emb_v, lsem.at[1]),
            pltpu.make_async_copy(proto_ref.at[:, ic], praw, lsem.at[2]),
        ]
        for load in loads:
            load.start()
        barrier = pltpu.get_barrier_semaphore()
        everyone = sorted(set(XZ + YC + XYC))
        for o in everyone:
            pl.semaphore_signal(barrier, inc=1, device_id=dev(o), device_id_type=MESH)

        loads[0].wait()
        pair = pair_v[...]
        lane = lax.broadcasted_iota(jnp.int32, (1, B), 1)
        first = (lane < pair).astype(F32)
        up = (
            lax.broadcasted_iota(jnp.int32, (B, B), 0) < lax.broadcasted_iota(jnp.int32, (B, B), 1)
        ).astype(F32).astype(BF16)
        rank = dot(jnp.broadcast_to(first, (8, B)).astype(BF16), up)[0:1, :]
        slot = jnp.where(first > 0.5, rank, -1.0).astype(jnp.int32)
        top = (lax.broadcasted_iota(jnp.int32, (HB, B), 0) == slot).astype(F32).astype(BF16)
        partner = (lax.broadcasted_iota(jnp.int32, (B, B), 0) == pair).astype(F32).astype(BF16)
        perm[0:HB, :] = top
        perm[HB:B, :] = dot(top, partner).astype(BF16)
        loads[1].wait()
        ep[...] = dot(perm[...], emb_v[...]).astype(BF16)
        uz, _ = unit(ep[...].astype(F32))
        zall[0, ic] = uz.astype(BF16)

        loads[2].wait()

        def norm_c(i, _):
            v = praw[pl.ds(i * (256 // OB), 256 // OB)].reshape(256, D).astype(F32)
            inv = 1.0 / jnp.sqrt(jnp.sum(v * v, axis=1, keepdims=True) + 1e-06)
            chat[pl.ds(pl.multiple_of(i * 256, 256), 256), :] = (v * inv).astype(BF16)
            return 0

        lax.fori_loop(0, NC // 256, norm_c, 0, unroll=2)

        def scores(h, js, fresh):
            rows = pl.ds(pl.multiple_of(h * B, B), B)
            zb = zall[0, h]
            for j in js:
                cols = slice(j * 256, (j + 1) * 256)
                e = jnp.exp(dot(zb, chat[cols, :], NT) * 10.0)
                E[rows, cols] = e
                k = e * e
                K[rows, cols] = k
                part = jnp.sum(k.reshape(B // 8, 8, 256), axis=0)
                colacc[:, cols] = part if fresh else colacc[:, cols] + part
                two = e[:, :128] + e[:, 128:]
                racc[rows, :] = two if j == 0 else racc[rows, :] + two

        NJ = NC // 256
        scores(ic, range(0, NJ - NJ // 4), True)
        pl.semaphore_wait(barrier, len(everyone))
        send(zall.at[0, ic], zall.at[0, ic], core_s, core_r, (0, 0, 1, 0))
        scores(ic, range(NJ - NJ // 4, NJ), True)
        take(zall.at[0, 1 - ic], core_r)
        scores(1 - ic, range(NJ), False)

        def col_send(t):
            for j in range(CC):
                crow[j : j + 1, :] = jnp.sum(colacc[:, j * 128 : (j + 1) * 128], axis=0, keepdims=True)
            csend[t] = crow[...].astype(BF16)
            for i, o in enumerate(XZ):
                send(csend.at[t], crecv.at[t, i + 1], cs.at[t], cr.at[t], o)
            pltpu.make_async_copy(csend.at[t], crecv.at[t, 0], cr.at[t]).start()

        def col_take(t):
            take(crecv.at[t], cr.at[t])
            crow[...] = 1.0 / jnp.sum(crecv[t].astype(F32), axis=0)

        def row_pass(out, keep):
            for i in range(RC):
                rows = slice(i * 128, (i + 1) * 128)
                acc = jnp.zeros((128, 128), F32)
                for j in range(CC):
                    w = K[rows, j * 128 : (j + 1) * 128] * crow[j : j + 1, :]
                    if keep:
                        K[rows, j * 128 : (j + 1) * 128] = w
                    acc = acc + w
                out[i : i + 1, :] = jnp.sum(acc.T, axis=0, keepdims=True)

        def col_pass():
            colacc[...] = jnp.zeros((8, NC), F32)

            def step(i, _):
                rows = pl.ds(pl.multiple_of(i * 128, 128), 128)
                r = rb[rows, :]
                for j in range(CC):
                    cols = slice(j * 128, (j + 1) * 128)
                    p = K[rows, cols] * r
                    colacc[:, cols] = colacc[:, cols] + jnp.sum(p.reshape(16, 8, 128), axis=0)
                return 0

            lax.fori_loop(0, RC, step, 0)

        def scores_t(a):
            mine = mine_c[...]
            for c in range(C):
                for q in range(B // 256):
                    n = (a * C + c) * (B // 256) + q
                    e = jnp.exp(dot(mine, zall[a, c, q * 256 : (q + 1) * 256, :], NT) * 10.0)
                    for half in range(2):
                        cols = slice(n * 256 + half * 128, n * 256 + (half + 1) * 128)
                        i = c * BC + q * 2 + half
                        eh = e[:, half * 128 : (half + 1) * 128]
                        WT[:, cols] = eh * eh
                        ET[:, cols] = eh * rp4[a, i : i + 1, :]

        def send_x(a):
            send(zall.at[0, ic], zall.at[a, ic], xs, xr.at[a], (a, 0, 0, 0))

        def forward(a):
            send(zall.at[a, ic], zall.at[a, ic], fs, fr.at[a], (0, 0, 1, 0))

        def relay(a, half):
            rows = pl.ds(half * HB, HB)
            send(zall.at[a, ic, rows], zall.at[FAR, ic, rows], xs, xr.at[FAR], (a, 0, 0, 0))

        col_send(0)
        for a in NEAR:
            send_x(a)
        for k, b in enumerate(FZ):
            mine_c[k * OB : (k + 1) * OB, :] = chat[pl.ds(pl.multiple_of(ix * TC + (iz + b) % Z * OB, OB), OB), :]
        for i in range(RC):
            rsend1[RC + i : RC + i + 1, :] = jnp.sum(racc[i * 128 : (i + 1) * 128, :].T, axis=0, keepdims=True)
        permt[...] = perm[...].astype(F32).T.astype(BF16)
        col_take(0)
        row_pass(rsend1, False)
        for i, o in enumerate(YC):
            send(rsend1, rrecv1.at[i + 1], rs.at[0], rr.at[0], o)
        pltpu.make_async_copy(rsend1, rrecv1.at[0], rr.at[0]).start()
        for half, a in enumerate(NEAR):
            take(zall.at[a, ic], xr.at[a])
            relay(a, half)
        for a in NEAR:
            forward(a)
        take(rrecv1, rr.at[0])
        totals = jnp.sum(rrecv1[...], axis=0)
        rrow[...] = 1.0 / totals[:RC, :]
        rp4[0] = 10.0 / totals[RC:, :]

        for i in range(RC):
            rb[i * 128 : (i + 1) * 128, :] = spread(rrow[i : i + 1, :])
        col_pass()
        col_send(1)
        for a in range(1, X):
            send(rp4.at[0], rp4.at[a], ps, pr.at[a], (a, 0, 0, 0))
        for i in range(RC):
            rpb[i * 128 : (i + 1) * 128, :] = spread(rp4[0, i : i + 1, :])
        scores_t(0)
        col_take(1)
        row_pass(rsend2, False)
        for i, o in enumerate(YC):
            send(rsend2, rrecv2.at[i + 1], rs.at[1], rr.at[1], o)
        pltpu.make_async_copy(rsend2, rrecv2.at[0], rr.at[1]).start()
        take(zall.at[FAR, ic], xr.at[FAR])
        forward(FAR)
        for a in NEAR:
            take(rp4.at[a], pr.at[a])
            take(zall.at[a, 1 - ic], fr.at[a])
            scores_t(a)
        take(rrecv2, rr.at[1])
        rrow[...] = 1.0 / jnp.sum(rrecv2[...], axis=0)

        for i in range(RC):
            rb[i * 128 : (i + 1) * 128, :] = spread(rrow[i : i + 1, :])
        col_pass()
        col_send(2)
        take(rp4.at[FAR], pr.at[FAR])
        take(zall.at[FAR, 1 - ic], fr.at[FAR])
        scores_t(FAR)
        col_take(2)
        row_pass(rsend3, True)
        for o in sorted(XYC, key=lambda o: o[0] != 0):
            send(rsend3, rrecv3.at[o[0] * GR + YCI[(0,) + o[1:]]], rs.at[2], rr.at[3 if o[0] else 2], o)
        pltpu.make_async_copy(rsend3, rrecv3.at[0], rr.at[2]).start()
        mine = crow[pl.ds(ix * (TC // 128), TC // 128), :]
        for i in range(TC // 128):
            c3a[i * 128 : (i + 1) * 128, :] = spread(mine[i : i + 1, :])
        for k, b in enumerate(FZ):
            c3b[k * OB : (k + 1) * OB, :] = c3a[pl.ds(pl.multiple_of((iz + b) % Z * OB, OB), OB), :]
        c3 = c3b[...]
        for n in range(X * RC):
            cols = slice(n * 128, (n + 1) * 128)
            WT[:, cols] = WT[:, cols] * c3
        take(rrecv3.at[pl.ds(0, GR)], rr.at[2])
        r34[0] = 10.0 / jnp.sum(rrecv3[0:GR], axis=0)
        for i in range(RC):
            rb[i * 128 : (i + 1) * 128, :] = spread(r34[0, i : i + 1, :])

        def grad_r(h):
            for q in range(2):
                rows = pl.ds(pl.multiple_of(h * B + q * HB, HB), HB)
                prows = pl.ds(pl.multiple_of(h * B + (1 - q) * HB, HB), HB)
                rp, r3 = rpb[rows, :], rb[prows, :]
                g = [
                    (E[rows, j * 128 : (j + 1) * 128] * rp - K[prows, j * 128 : (j + 1) * 128] * r3).astype(BF16)
                    for j in range(CC)
                ]
                yield q, dot(jnp.concatenate(g, axis=1), chat[...])

        for q, part in grad_r(1 - ic):
            ksend[q] = part.astype(BF16)
        for q in range(2):
            send(ksend.at[q], krecv.at[q], ks.at[q], kr.at[q], (0, 0, 1, 0))
        for q, part in grad_r(ic):
            gpart[q] = part
        far_y = sorted(range(1, Y), key=lambda k: -ring(k, Y))
        for q in range(2):
            take(krecv.at[q], kr.at[q])
            gpart[q] = gpart[q] + krecv[q].astype(F32)
            ysend[q] = gpart[q].reshape(Y, HB // Y, D).astype(BF16)
            for f in far_y:
                send(ysend.at[q, (iy + f) % Y], yrecv.at[q, f - 1], ys.at[q], yr.at[q], (0, 0, 0, f))

        take(rrecv3.at[pl.ds(GR, (X - 1) * GR)], rr.at[3])
        for a in range(1, X):
            r34[a] = 10.0 / jnp.sum(rrecv3[a * GR : (a + 1) * GR], axis=0)
        for n in range(X * C):
            a, c = n // C, n % C
            g = []
            for q in range(BC):
                qp = (q + BC // 2) % BC
                cols = slice(n * B + q * 128, n * B + (q + 1) * 128)
                pcols = slice(n * B + qp * 128, n * B + (qp + 1) * 128)
                r3 = r34[a, c * BC + qp : c * BC + qp + 1, :]
                g.append((ET[:, cols] - WT[:, pcols] * r3).astype(BF16))
            part = dot(jnp.concatenate(g, axis=1), zall[a, c])
            tpart[...] = part if n == 0 else tpart[...] + part
        zsend[...] = tpart[0 : (Z - 1) * OB, :].reshape(Z - 1, OB, D).astype(BF16)
        for k in range(Z - 1):
            send(zsend.at[k], zrecv.at[k], zs, zr, (0, FZ[k], 0, 0))

        SB = HB // Y
        for q in range(2):
            take(yrecv.at[q], yr.at[q])
            at = pl.ds(pl.multiple_of(iy * SB, SB), SB)
            gzs = gpart[q, at, :] + jnp.sum(yrecv[q].astype(F32), axis=0)
            uq, nq = unit(ep[pl.ds(pl.multiple_of(q * HB + iy * SB, SB), SB), :].astype(F32))
            yall[q, iy] = ((gzs - uq * jnp.sum(uq * gzs, axis=1, keepdims=True)) / nq).astype(BF16)
            for f in far_y:
                send(yall.at[q, iy], yall.at[q, iy], gs.at[q], gr.at[q], (0, 0, 0, f))

        take(zrecv, zr)
        gcs = tpart[(Z - 1) * OB : Z * OB, :] + jnp.sum(zrecv[...].astype(F32), axis=0)
        uc, nc = unit(praw[ix * Z + iz].astype(F32))
        gc_ref[...] = (gcs - uc * jnp.sum(uc * gcs, axis=1, keepdims=True)) / nc
        for q in range(2):
            take(yall.at[q, pl.ds(0, Y - 1)], gr.at[q])
        gz_ref[...] = dot(permt[...], yall[...].reshape(B, D))

        take(zall.at[0, ic], core_s)
        take(zall.at[pl.ds(0, X - 1), 0], xs)
        take(zall.at[pl.ds(0, X - 1), 0], fs)
        take(rp4.at[pl.ds(0, X - 1)], ps)
        for t in range(3):
            take(crecv.at[t, pl.ds(0, len(XZ))], cs.at[t])
        take(rrecv1.at[pl.ds(0, len(YC))], rs.at[0])
        take(rrecv2.at[pl.ds(0, len(YC))], rs.at[1])
        take(rrecv3.at[pl.ds(0, len(XYC))], rs.at[2])
        take(zrecv, zs)
        for q in range(2):
            take(ksend.at[q], ks.at[q])
            take(yrecv.at[q], ys.at[q])
            take(yall.at[q, pl.ds(0, Y - 1)], gs.at[q])

    V = pltpu.VMEM
    S = pltpu.SemaphoreType.DMA
    scratch = [
        V((1, B), jnp.int32),
        V((B, D), BF16),
        V((X * Z, OB, D), BF16),
        V((NC, D), BF16),
        V((B, D), BF16),
        V((B, B), BF16),
        V((B, B), BF16),
        V((X, C, B, D), BF16),
        V((RT, NC), F32),
        V((RT, NC), F32),
        V((TC, X * RT), F32),
        V((TC, X * RT), F32),
        V((8, NC), F32),
        V((RT, 128), F32),
        V((RT, 128), F32),
        V((RT, 128), F32),
        V((TC, 128), F32),
        V((TC, 128), F32),
        V((TC, D), BF16),
        V((CC, 128), F32),
        V((RC, 128), F32),
        V((X, RC, 128), F32),
        V((X, RC, 128), F32),
        V((3, CC, 128), BF16),
        V((3, len(XZ) + 1, CC, 128), BF16),
        V((2 * RC, 128), F32),
        V((len(YC) + 1, 2 * RC, 128), F32),
        V((RC, 128), F32),
        V((len(YC) + 1, RC, 128), F32),
        V((RC, 128), F32),
        V((X * (len(YC) + 1), RC, 128), F32),
        V((2, HB, D), F32),
        V((2, HB, D), BF16),
        V((2, HB, D), BF16),
        V((TC, D), F32),
        V((Z - 1, OB, D), BF16),
        V((Z - 1, OB, D), BF16),
        V((2, Y, HB // Y, D), BF16),
        V((2, Y - 1, HB // Y, D), BF16),
        V((2, Y, HB // Y, D), BF16),
        S((3,)),
        S, S,
        S, S((X,)),
        S, S((X,)),
        S((3,)), S((3,)),
        S((3,)), S((4,)),
        S, S((X,)),
        S((2,)), S((2,)),
        S, S,
        S((2,)), S((2,)),
        S((2,)), S((2,)),
    ]
    return kernel, scratch


def place(gz_ref, gc_ref, gz_out, gc_out):
    gz_out[...] = gz_ref[...]
    gc_out[...] = gc_ref[...]


def body(embeddings, prototypes, pair_index):
    B, D = embeddings.shape
    NCL = prototypes.shape[0]
    NC = NCL // C
    OB = NCL // (X * Z * C)
    kernel, scratch = make_kernel(B, D, NC)
    vm = pl.BlockSpec(memory_space=pltpu.VMEM)
    hbm = pl.BlockSpec(memory_space=pl.ANY)
    shapes = (jax.ShapeDtypeStruct((B, D), F32), jax.ShapeDtypeStruct((OB, D), F32))
    grads = pl.pallas_call(
        kernel,
        out_shape=shapes,
        in_specs=[hbm, hbm, hbm],
        out_specs=(vm, vm),
        scratch_shapes=scratch,
        compiler_params=pltpu.CompilerParams(
            collective_id=0, has_side_effects=True, vmem_limit_bytes=60 * 2**20
        ),
        name="swav",
    )(embeddings, prototypes.reshape(X * Z, C, OB, D), pair_index.reshape(1, B))
    return pl.pallas_call(
        place,
        out_shape=shapes,
        in_specs=[vm, vm],
        out_specs=(vm, vm),
        name="place",
    )(*grads)


def solution(mesh):
    return jax.shard_map(
        body,
        mesh=mesh,
        in_specs=(P("dp", None), P("proto", None), P("dp")),
        out_specs=(P("dp", None), P(("proto", "dp"), None)),
        check_vma=False,
    )
```

```python
import jax
import jax.numpy as jnp
from jax import lax
from jax.experimental import pallas as pl
from jax.experimental.pallas import tpu as pltpu
from jax.sharding import PartitionSpec as P

X, Z, C, Y = 4, 8, 2, 4
MESH = pl.DeviceIdType.MESH
F32, BF16 = jnp.float32, jnp.bfloat16
NT = (((1,), (1,)), ((), ()))
NN = (((1,), (0,)), ((), ()))


def ring(k, n):
    return min(k, n - k)


def offsets(axes):
    span = [n if a in axes else 1 for a, n in zip("xzcy", (X, Z, C, Y))]
    out = [
        (a, b, e, f)
        for a in range(span[0])
        for b in range(span[1])
        for e in range(span[2])
        for f in range(span[3])
        if a or b or e or f
    ]
    return sorted(out, key=farthest)


def farthest(t):
    return -(4 * (ring(t[0], X) + ring(t[1], Z) + ring(t[3], Y)) + t[2])


def dot(a, b, dims=NN):
    return lax.dot_general(a, b, dims, preferred_element_type=F32)


def unit(values):
    norm = jnp.sqrt(jnp.sum(values * values, axis=1, keepdims=True) + 1e-06)
    return values / norm, norm


def spread(row):
    return jnp.broadcast_to(row, (128, 128)).T


def make_kernel(B, D, NC):
    RT, RC, CC, TC = C * B, C * B // 128, NC // 128, NC // X
    OB = TC // Z
    BC = B // 128
    HB = B // 2
    FZ = [Z // 2 + k // 2 if k % 2 == 0 else Z // 2 - (k + 1) // 2 for k in range(Z)]
    NEAR, FAR = (1, X - 1), 2
    XZ, YC, XYC = offsets("xz"), offsets("yc"), offsets("xyc")

    GR = len(YC) + 1
    YCI = {o: i + 1 for i, o in enumerate(YC)}
    YCI[(0, 0, 0, 0)] = 0

    def kernel(
        emb_ref, proto_ref, pair_ref, gz_ref, gc_ref,
        pair_v, emb_v, zu, praw, chat, chato, ep, perm, permt, zall, E, K, ET, WT, colacc, racc, rb, rpb, c3a, c3b, mine_c,
        crow, rrow, rp4, r34, csend, crecv, fsend, frecv, tsend, trecv, rsend, rrecv, rsend3, rrecv3,
        gpart, ksend, krecv, tpart, zsend, zrecv, ysend, yrecv, yall,
        lsem, core_s, core_r, xs, xr, fs, fr, cs, cr, f_s, f_r, ts, tr, rs, rr, ps, pr, ks, kr, zs, zr, ys, yr, gs, gr,
    ):
        dp = lax.axis_index("dp")
        iy = lax.axis_index("proto")
        ix, iz, ic = dp // (Z * C), (dp // C) % Z, dp % C

        def dev(o):
            a, b, e, f = o
            nx = (ix + a) % X if a else ix
            nz = (iz + b) % Z if b else iz
            nc = (ic + e) % C if e else ic
            ny = (iy + f) % Y if f else iy
            return {"dp": (nx * Z + nz) * C + nc, "proto": ny}

        def send(src, dst, s, r, o):
            pltpu.make_async_remote_copy(
                src_ref=src, dst_ref=dst, send_sem=s, recv_sem=r, device_id=dev(o), device_id_type=MESH
            ).start()

        def take(ref, sem):
            pltpu.make_async_copy(ref, ref, sem).wait()

        loads = [
            pltpu.make_async_copy(pair_ref, pair_v, lsem.at[0]),
            pltpu.make_async_copy(emb_ref, emb_v, lsem.at[1]),
            pltpu.make_async_copy(proto_ref, praw, lsem.at[2]),
        ]
        for load in loads:
            load.start()
        barrier = pltpu.get_barrier_semaphore()
        everyone = sorted(sorted(set(XZ + YC + XYC)), key=farthest)
        for o in everyone:
            pl.semaphore_signal(barrier, inc=1, device_id=dev(o), device_id_type=MESH)

        loads[1].wait()
        loads[0].wait()
        v = emb_v[...].astype(F32)
        zu[...] = (v * (1.0 / jnp.sqrt(jnp.sum(v * v, axis=1, keepdims=True) + 1e-06))).astype(BF16)
        loads[2].wait()
        NB = 256 // OB

        def norm_c(half, out):
            def step(i, _):
                v = praw[pl.ds(i * NB, NB), half].reshape(256, D).astype(F32)
                inv = 1.0 / jnp.sqrt(jnp.sum(v * v, axis=1, keepdims=True) + 1e-06)
                out[pl.ds(pl.multiple_of(i * 256, 256), 256), :] = (v * inv).astype(BF16)
                return 0

            lax.fori_loop(0, NC // 256, step, 0, unroll=2)

        def first_totals(prototypes, out):
            zb = zu[...]
            for j in range(NC // 256):
                k = jnp.exp(dot(zb, prototypes[j * 256 : (j + 1) * 256, :], NT) * 20.0)
                colacc[:, j * 256 : (j + 1) * 256] = jnp.sum(k.reshape(B // 8, 8, 256), axis=0)
            for j in range(CC):
                out[j : j + 1, :] = jnp.sum(colacc[:, j * 128 : (j + 1) * 128], axis=0, keepdims=True)

        norm_c(1 - ic, chato)
        norm_c(ic, chat)
        first_totals(chato, fsend)
        pl.semaphore_wait(barrier, len(everyone))
        send(fsend, frecv, f_s, f_r, (0, 0, 1, 0))
        first_totals(chat, crow)

        def reorder():
            pair = pair_v[...]
            lane = lax.broadcasted_iota(jnp.int32, (1, B), 1)
            first = (lane < pair).astype(F32)
            up = (
                lax.broadcasted_iota(jnp.int32, (B, B), 0) < lax.broadcasted_iota(jnp.int32, (B, B), 1)
            ).astype(F32).astype(BF16)
            rank = dot(jnp.broadcast_to(first, (8, B)).astype(BF16), up)[0:1, :]
            slot = jnp.where(first > 0.5, rank, -1.0).astype(jnp.int32)
            top = (lax.broadcasted_iota(jnp.int32, (HB, B), 0) == slot).astype(F32).astype(BF16)
            partner = (lax.broadcasted_iota(jnp.int32, (B, B), 0) == pair).astype(F32).astype(BF16)
            perm[0:HB, :] = top
            perm[HB:B, :] = dot(top, partner).astype(BF16)
            ep[...] = dot(perm[...], emb_v[...]).astype(BF16)
            uz, _ = unit(ep[...].astype(F32))
            zall[0, ic] = uz.astype(BF16)

        def scores(h, js):
            rows = pl.ds(pl.multiple_of(h * B, B), B)
            zb = zall[0, h]
            for j in js:
                cols = slice(j * 256, (j + 1) * 256)
                e = jnp.exp(dot(zb, chat[cols, :], NT) * 10.0)
                E[rows, cols] = e
                k = e * e
                K[rows, cols] = k
                two = e[:, :128] + e[:, 128:]
                racc[rows, :] = two if j == 0 else racc[rows, :] + two

        def col_send(t):
            if t:
                for j in range(CC):
                    crow[j : j + 1, :] = jnp.sum(colacc[:, j * 128 : (j + 1) * 128], axis=0, keepdims=True)
            csend[t] = crow[...].astype(BF16)
            for i, o in enumerate(XZ):
                send(csend.at[t], crecv.at[t, i + 1], cs.at[t], cr.at[t], o)
            pltpu.make_async_copy(csend.at[t], crecv.at[t, 0], cr.at[t]).start()

        def col_take(t):
            take(crecv.at[t], cr.at[t])
            crow[...] = 1.0 / jnp.sum(crecv[t].astype(F32), axis=0)

        def row_pass(out, blocks, keep):
            for i in range(blocks[0] * BC, (blocks[-1] + 1) * BC):
                rows = slice(i * 128, (i + 1) * 128)
                acc = jnp.zeros((128, 128), F32)
                for j in range(CC):
                    w = K[rows, j * 128 : (j + 1) * 128] * crow[j : j + 1, :]
                    if keep:
                        K[rows, j * 128 : (j + 1) * 128] = w
                    acc = acc + w
                out[i // BC, i % BC : i % BC + 1, :] = jnp.sum(acc.T, axis=0, keepdims=True)

        def col_pass(t):
            for blk in range(C):
                take(rrecv.at[t, blk], rr.at[t * C + blk])
                rrow[...] = 1.0 / jnp.sum(rrecv[t, blk], axis=0)
                for i in range(BC):
                    rb[i * 128 : (i + 1) * 128, :] = spread(rrow[i : i + 1, :])

                for jg in range(0, CC, 8):
                    acc = [jnp.zeros((8, 128), F32) for _ in range(8)]
                    for i in range(BC):
                        r = rb[i * 128 : (i + 1) * 128, :]
                        rows = slice(blk * B + i * 128, blk * B + (i + 1) * 128)
                        for j in range(8):
                            p = K[rows, (jg + j) * 128 : (jg + j + 1) * 128] * r
                            acc[j] = acc[j] + jnp.sum(p.reshape(16, 8, 128), axis=0)
                    for j in range(8):
                        cols = slice((jg + j) * 128, (jg + j + 1) * 128)
                        colacc[:, cols] = colacc[:, cols] + acc[j] if blk else acc[j]

        def row_send(t):
            for blk in range(C):
                row_pass(rsend.at[t], (blk,), False)
                for i, o in enumerate(YC):
                    send(rsend.at[t, blk], rrecv.at[t, blk, i + 1], rs.at[t * C + blk], rr.at[t * C + blk], o)
                pltpu.make_async_copy(rsend.at[t, blk], rrecv.at[t, blk, 0], rr.at[t * C + blk]).start()

        def scores_t(a):
            mine = mine_c[...]
            for c in range(C):
                for q in range(B // 256):
                    n = (a * C + c) * (B // 256) + q
                    e = jnp.exp(dot(mine, zall[a, c, q * 256 : (q + 1) * 256, :], NT) * 10.0)
                    for half in range(2):
                        cols = slice(n * 256 + half * 128, n * 256 + (half + 1) * 128)
                        i = c * BC + q * 2 + half
                        eh = e[:, half * 128 : (half + 1) * 128]
                        WT[:, cols] = eh * eh
                        ET[:, cols] = eh * rp4[a, i : i + 1, :]

        def send_x(a):
            send(zall.at[0, ic], zall.at[a, ic], xs, xr.at[a], (a, 0, 0, 0))

        def forward(a):
            send(zall.at[a, ic], zall.at[a, ic], fs, fr.at[a], (0, 0, 1, 0))

        def relay(a, half):
            rows = pl.ds(half * HB, HB)
            send(zall.at[a, ic, rows], zall.at[FAR, ic, rows], xs, xr.at[FAR], (a, 0, 0, 0))

        take(frecv, f_r)
        crow[...] = crow[...] + frecv[...]
        col_send(0)
        reorder()
        send(zall.at[0, ic], zall.at[0, ic], core_s, core_r, (0, 0, 1, 0))
        for a in NEAR:
            send_x(a)
        scores(ic, range(NC // 256))
        take(zall.at[0, 1 - ic], core_r)
        scores(1 - ic, range(NC // 256))
        for i in range(RC):
            tsend[i : i + 1, :] = jnp.sum(racc[i * 128 : (i + 1) * 128, :].T, axis=0, keepdims=True)
        for i, o in enumerate(YC):
            send(tsend, trecv.at[i + 1], ts, tr, o)
        pltpu.make_async_copy(tsend, trecv.at[0], tr).start()
        col_take(0)
        row_send(0)
        permt[...] = perm[...].astype(F32).T.astype(BF16)
        for k, b in enumerate(FZ):
            mine_c[k * OB : (k + 1) * OB, :] = chat[pl.ds(pl.multiple_of(ix * TC + (iz + b) % Z * OB, OB), OB), :]
        take(trecv, tr)
        rp4[0] = 10.0 / jnp.sum(trecv[...], axis=0)
        for a in range(1, X):
            send(rp4.at[0], rp4.at[a], ps, pr.at[a], (a, 0, 0, 0))
        for half, a in enumerate(NEAR):
            take(zall.at[a, ic], xr.at[a])
            relay(a, half)
        for a in NEAR:
            forward(a)

        col_pass(0)
        col_send(1)
        for i in range(RC):
            rpb[i * 128 : (i + 1) * 128, :] = spread(rp4[0, i : i + 1, :])

        def scale(i, _):
            rows = pl.ds(pl.multiple_of(i * 64, 64), 64)
            rp = rpb[rows, :]
            for j in range(CC):
                E[rows, j * 128 : (j + 1) * 128] = E[rows, j * 128 : (j + 1) * 128] * rp
            return 0

        lax.fori_loop(0, RT // 64, scale, 0)
        scores_t(0)
        col_take(1)
        row_send(1)
        take(zall.at[FAR, ic], xr.at[FAR])
        forward(FAR)
        for a in NEAR:
            take(rp4.at[a], pr.at[a])
            take(zall.at[a, 1 - ic], fr.at[a])
            scores_t(a)

        col_pass(1)
        col_send(2)
        take(rp4.at[FAR], pr.at[FAR])
        take(zall.at[FAR, 1 - ic], fr.at[FAR])
        scores_t(FAR)
        col_take(2)
        row_pass(rsend3, range(C), True)
        for o in sorted(XYC, key=lambda o: o[0] != 0):
            send(rsend3, rrecv3.at[o[0] * GR + YCI[(0,) + o[1:]]], rs.at[4], rr.at[5 if o[0] else 4], o)
        pltpu.make_async_copy(rsend3, rrecv3.at[0], rr.at[4]).start()
        mine = crow[pl.ds(ix * (TC // 128), TC // 128), :]
        for i in range(TC // 128):
            c3a[i * 128 : (i + 1) * 128, :] = spread(mine[i : i + 1, :])
        for k, b in enumerate(FZ):
            c3b[k * OB : (k + 1) * OB, :] = c3a[pl.ds(pl.multiple_of((iz + b) % Z * OB, OB), OB), :]
        c3 = c3b[...]
        for n in range(X * RC):
            cols = slice(n * 128, (n + 1) * 128)
            WT[:, cols] = WT[:, cols] * c3
        take(rrecv3.at[pl.ds(0, GR)], rr.at[4])
        r34[0] = 10.0 / jnp.sum(rrecv3[0:GR], axis=0).reshape(RC, 128)
        for i in range(RC):
            rb[i * 128 : (i + 1) * 128, :] = spread(r34[0, i : i + 1, :])

        def grad_r(h, out):
            for q in range(2):
                rows = pl.ds(pl.multiple_of(h * B + q * HB, HB), HB)
                prows = pl.ds(pl.multiple_of(h * B + (1 - q) * HB, HB), HB)
                r3 = rb[prows, :]
                g = [
                    (E[rows, j * 128 : (j + 1) * 128] - K[prows, j * 128 : (j + 1) * 128] * r3).astype(BF16)
                    for j in range(CC)
                ]
                out[q] = dot(jnp.concatenate(g, axis=1), chat[...]).astype(out.dtype)

        grad_r(1 - ic, ksend)
        for q in range(2):
            send(ksend.at[q], krecv.at[q], ks.at[q], kr.at[q], (0, 0, 1, 0))
        grad_r(ic, gpart)
        take(rrecv3.at[pl.ds(GR, (X - 1) * GR)], rr.at[5])
        for a in range(1, X):
            r34[a] = 10.0 / jnp.sum(rrecv3[a * GR : (a + 1) * GR], axis=0).reshape(RC, 128)
        far_y = sorted(range(1, Y), key=lambda k: -ring(k, Y))
        for q in range(2):
            take(krecv.at[q], kr.at[q])
            gpart[q] = gpart[q] + krecv[q].astype(F32)
            ysend[q] = gpart[q].reshape(Y, HB // Y, D).astype(BF16)
            for f in far_y:
                send(ysend.at[q, (iy + f) % Y], yrecv.at[q, f - 1], ys.at[q], yr.at[q], (0, 0, 0, f))

        HT, ZH = TC // 2, Z // 2

        def grad_t(m, _):
            rows = pl.ds(pl.multiple_of(m * HT, HT), HT)
            g = []
            for n in range(X * RC):
                a, q = n // RC, n % RC
                qp = q // BC * BC + (q + BC // 2) % BC
                cols, pcols = slice(n * 128, (n + 1) * 128), slice((a * RC + qp) * 128, (a * RC + qp + 1) * 128)
                g.append((ET[rows, cols] - WT[rows, pcols] * r34[a, qp : qp + 1, :]).astype(BF16))
            part = dot(jnp.concatenate(g, axis=1), zall[...].reshape(X * RT, D))
            tpart[rows, :] = part
            zsend[pl.ds(m * ZH, ZH)] = part.reshape(ZH, OB, D).astype(BF16)
            for k in range(ZH):
                b = Z // 2 + m * (ZH // 2) + k // 2 if k % 2 == 0 else Z // 2 - m * (ZH // 2) - (k + 1) // 2
                to = {"dp": (ix * Z + (iz + b) % Z) * C + ic, "proto": iy}

                def go(k=k, to=to):
                    pltpu.make_async_remote_copy(
                        src_ref=zsend.at[m * ZH + k], dst_ref=zrecv.at[m * ZH + k], send_sem=zs, recv_sem=zr,
                        device_id=to, device_id_type=MESH,
                    ).start()

                if k < ZH - 1:
                    go()
                else:
                    pl.when(m == 0)(go)
            return 0

        lax.fori_loop(0, 2, grad_t, 0)

        SB = HB // Y
        for q in range(2):
            take(yrecv.at[q], yr.at[q])
            at = pl.ds(pl.multiple_of(iy * SB, SB), SB)
            gzs = gpart[q, at, :] + jnp.sum(yrecv[q].astype(F32), axis=0)
            uq, nq = unit(ep[pl.ds(pl.multiple_of(q * HB + iy * SB, SB), SB), :].astype(F32))
            yall[q, iy] = ((gzs - uq * jnp.sum(uq * gzs, axis=1, keepdims=True)) / nq).astype(BF16)
            for f in far_y:
                send(yall.at[q, iy], yall.at[q, iy], gs.at[q], gr.at[q], (0, 0, 0, f))

        take(zrecv, zr)
        gcs = tpart[(Z - 1) * OB : Z * OB, :] + jnp.sum(zrecv[...].astype(F32), axis=0)
        uc, nc = unit(praw[ix * Z + iz, ic].astype(F32))
        gc_ref[...] = (gcs - uc * jnp.sum(uc * gcs, axis=1, keepdims=True)) / nc
        for q in range(2):
            take(yall.at[q, pl.ds(0, Y - 1)], gr.at[q])
        gz_ref[...] = dot(permt[...], yall[...].reshape(B, D))

        take(zall.at[0, ic], core_s)
        take(zall.at[pl.ds(0, X - 1), 0], xs)
        take(zall.at[pl.ds(0, X - 1), 0], fs)
        take(rp4.at[pl.ds(0, X - 1)], ps)
        for t in range(3):
            take(crecv.at[t, pl.ds(0, len(XZ))], cs.at[t])
        take(fsend, f_s)
        take(trecv.at[pl.ds(0, len(YC))], ts)
        for t in range(2):
            for blk in range(C):
                take(rrecv.at[t, blk, pl.ds(0, len(YC))], rs.at[t * C + blk])
        take(rrecv3.at[pl.ds(0, len(XYC))], rs.at[4])
        take(zrecv, zs)
        for q in range(2):
            take(ksend.at[q], ks.at[q])
            take(yrecv.at[q], ys.at[q])
            take(yall.at[q, pl.ds(0, Y - 1)], gs.at[q])

    V = pltpu.VMEM
    S = pltpu.SemaphoreType.DMA
    scratch = [
        V((1, B), jnp.int32),
        V((B, D), BF16),
        V((B, D), BF16),
        V((X * Z, C, OB, D), BF16),
        V((NC, D), BF16),
        V((NC, D), BF16),
        V((B, D), BF16),
        V((B, B), BF16),
        V((B, B), BF16),
        V((X, C, B, D), BF16),
        V((RT, NC), F32),
        V((RT, NC), F32),
        V((TC, X * RT), F32),
        V((TC, X * RT), F32),
        V((8, NC), F32),
        V((RT, 128), F32),
        V((RT, 128), F32),
        V((RT, 128), F32),
        V((TC, 128), F32),
        V((TC, 128), F32),
        V((TC, D), BF16),
        V((CC, 128), F32),
        V((BC, 128), F32),
        V((X, RC, 128), F32),
        V((X, RC, 128), F32),
        V((3, CC, 128), BF16),
        V((3, len(XZ) + 1, CC, 128), BF16),
        V((CC, 128), F32),
        V((CC, 128), F32),
        V((RC, 128), F32),
        V((GR, RC, 128), F32),
        V((2, C, BC, 128), F32),
        V((2, C, GR, BC, 128), F32),
        V((C, BC, 128), F32),
        V((X * GR, C, BC, 128), F32),
        V((2, HB, D), F32),
        V((2, HB, D), BF16),
        V((2, HB, D), BF16),
        V((TC, D), F32),
        V((Z, OB, D), BF16),
        V((Z - 1, OB, D), BF16),
        V((2, Y, HB // Y, D), BF16),
        V((2, Y - 1, HB // Y, D), BF16),
        V((2, Y, HB // Y, D), BF16),
        S((3,)),
        S, S,
        S, S((X,)),
        S, S((X,)),
        S((3,)), S((3,)),
        S, S,
        S, S,
        S((5,)), S((6,)),
        S, S((X,)),
        S((2,)), S((2,)),
        S, S,
        S((2,)), S((2,)),
        S((2,)), S((2,)),
    ]
    return kernel, scratch


def place(gz_ref, gc_ref, gz_out, gc_out, sem):
    copies = [
        pltpu.make_async_copy(gz_ref, gz_out, sem.at[0]),
        pltpu.make_async_copy(gc_ref, gc_out, sem.at[1]),
    ]
    for copy in copies:
        copy.start()
    for copy in copies:
        copy.wait()


def body(embeddings, prototypes, pair_index):
    B, D = embeddings.shape
    NCL = prototypes.shape[0]
    NC = NCL // C
    OB = NCL // (X * Z * C)
    kernel, scratch = make_kernel(B, D, NC)
    vm = pl.BlockSpec(memory_space=pltpu.VMEM)
    hbm = pl.BlockSpec(memory_space=pl.ANY)
    shapes = (jax.ShapeDtypeStruct((B, D), F32), jax.ShapeDtypeStruct((OB, D), F32))
    held = (pltpu.VMEM((B, D), F32), pltpu.VMEM((OB, D), F32))
    grads = pl.pallas_call(
        kernel,
        out_shape=held,
        in_specs=[hbm, hbm, hbm],
        out_specs=(vm, vm),
        scratch_shapes=scratch,
        compiler_params=pltpu.CompilerParams(
            collective_id=0, has_side_effects=True, vmem_limit_bytes=60 * 2**20
        ),
        name="swav",
    )(embeddings, prototypes.reshape(X * Z, C, OB, D), pair_index.reshape(1, B))
    return pl.pallas_call(
        place,
        out_shape=shapes,
        in_specs=[vm, vm],
        out_specs=(hbm, hbm),
        scratch_shapes=[pltpu.SemaphoreType.DMA((2,))],
        name="place",
    )(*(pltpu.with_memory_space_constraint(g, pltpu.VMEM) for g in grads))


def solution(mesh):
    return jax.shard_map(
        body,
        mesh=mesh,
        in_specs=(P("dp", None), P("proto", None), P("dp")),
        out_specs=(P("dp", None), P(("proto", "dp"), None)),
        check_vma=False,
    )
```

```python
import jax
import jax.numpy as jnp
from jax import lax
from jax.experimental import pallas as pl
from jax.experimental.pallas import tpu as pltpu
from jax.sharding import PartitionSpec as P

X, Z, C, Y = 4, 8, 2, 4
MESH = pl.DeviceIdType.MESH
F32, BF16 = jnp.float32, jnp.bfloat16
NT = (((1,), (1,)), ((), ()))
NN = (((1,), (0,)), ((), ()))


def ring(k, n):
    return min(k, n - k)


def offsets(axes):
    span = [n if a in axes else 1 for a, n in zip("xzcy", (X, Z, C, Y))]
    out = [
        (a, b, e, f)
        for a in range(span[0])
        for b in range(span[1])
        for e in range(span[2])
        for f in range(span[3])
        if a or b or e or f
    ]
    return sorted(out, key=farthest)


def farthest(t):
    return -(4 * (ring(t[0], X) + ring(t[1], Z) + ring(t[3], Y)) + t[2])


def dot(a, b, dims=NN):
    return lax.dot_general(a, b, dims, preferred_element_type=F32)


def unit(values):
    norm = jnp.sqrt(jnp.sum(values * values, axis=1, keepdims=True) + 1e-06)
    return values / norm, norm


def spread(row):
    return jnp.broadcast_to(row, (128, 128)).T


def make_kernel(B, D, NC):
    RT, RC, CC, TC = C * B, C * B // 128, NC // 128, NC // X
    OB = TC // Z
    BC = B // 128
    HB = B // 2
    FZ = [Z // 2 + k // 2 if k % 2 == 0 else Z // 2 - (k + 1) // 2 for k in range(Z)]
    NEAR, FAR = (1, X - 1), 2
    XZ, YC, XYC = offsets("xz"), offsets("yc"), offsets("xyc")

    GR = len(YC) + 1
    YCI = {o: i + 1 for i, o in enumerate(YC)}
    YCI[(0, 0, 0, 0)] = 0

    def kernel(
        emb_ref, proto_ref, pair_ref, gz_ref, gc_ref,
        pair_v, emb_v, zu, praw, chat, chato, ep, perm, permt, zall, K, KT, P1, precv, pown, TP, U, urecv, colacc, racc, rb, c3a, c3b, mine_c,
        crow, rrow, rp4, r34, csend, crecv, fsend, frecv, tsend, trecv, rsend, rrecv, rsend3, rrecv3,
        gpart, tpart, zsend, zrecv, ysend, yrecv, yall,
        lsem, core_s, core_r, xs, xr, fs, fr, cs, cr, f_s, f_r, ts, tr, rs, rr, ps, pr, p_s, p_r, ks, kr, zs, zr, ys, yr, gs, gr,
    ):
        dp = lax.axis_index("dp")
        iy = lax.axis_index("proto")
        ix, iz, ic = dp // (Z * C), (dp // C) % Z, dp % C

        def dev(o):
            a, b, e, f = o
            nx = (ix + a) % X if a else ix
            nz = (iz + b) % Z if b else iz
            nc = (ic + e) % C if e else ic
            ny = (iy + f) % Y if f else iy
            return {"dp": (nx * Z + nz) * C + nc, "proto": ny}

        def send(src, dst, s, r, o):
            pltpu.make_async_remote_copy(
                src_ref=src, dst_ref=dst, send_sem=s, recv_sem=r, device_id=dev(o), device_id_type=MESH
            ).start()

        def take(ref, sem):
            pltpu.make_async_copy(ref, ref, sem).wait()

        loads = [
            pltpu.make_async_copy(pair_ref, pair_v, lsem.at[0]),
            pltpu.make_async_copy(emb_ref, emb_v, lsem.at[1]),
            pltpu.make_async_copy(proto_ref.at[:, 1 - ic], praw.at[1], lsem.at[2]),
            pltpu.make_async_copy(proto_ref.at[:, ic], praw.at[0], lsem.at[3]),
        ]
        for load in loads:
            load.start()
        barrier = pltpu.get_barrier_semaphore()
        everyone = sorted(sorted(set(XZ + YC + XYC)), key=farthest)
        for o in everyone:
            pl.semaphore_signal(barrier, inc=1, device_id=dev(o), device_id_type=MESH)

        loads[1].wait()
        loads[0].wait()
        v = emb_v[...].astype(F32)
        zu[...] = (v * (1.0 / jnp.sqrt(jnp.sum(v * v, axis=1, keepdims=True) + 1e-06))).astype(BF16)
        NB = 256 // OB

        def norm_c(half, out):
            def step(i, _):
                v = praw[half, pl.ds(i * NB, NB)].reshape(256, D).astype(F32)
                inv = 1.0 / jnp.sqrt(jnp.sum(v * v, axis=1, keepdims=True) + 1e-06)
                out[pl.ds(pl.multiple_of(i * 256, 256), 256), :] = (v * inv).astype(BF16)
                return 0

            lax.fori_loop(0, NC // 256, step, 0, unroll=2)

        def first_totals(prototypes, out):
            zb = zu[...]
            for j in range(NC // 256):
                k = jnp.exp(dot(zb, prototypes[j * 256 : (j + 1) * 256, :], NT) * 20.0)
                colacc[:, j * 256 : (j + 1) * 256] = jnp.sum(k.reshape(B // 8, 8, 256), axis=0)
            for j in range(CC):
                out[j : j + 1, :] = jnp.sum(colacc[:, j * 128 : (j + 1) * 128], axis=0, keepdims=True)

        loads[2].wait()
        norm_c(1, chato)
        first_totals(chato, fsend)
        loads[3].wait()
        norm_c(0, chat)
        pl.semaphore_wait(barrier, len(everyone))
        send(fsend, frecv, f_s, f_r, (0, 0, 1, 0))
        first_totals(chat, crow)

        def reorder():
            pair = pair_v[...]
            lane = lax.broadcasted_iota(jnp.int32, (1, B), 1)
            first = (lane < pair).astype(F32)
            up = (
                lax.broadcasted_iota(jnp.int32, (B, B), 0) < lax.broadcasted_iota(jnp.int32, (B, B), 1)
            ).astype(F32).astype(BF16)
            rank = dot(jnp.broadcast_to(first, (8, B)).astype(BF16), up)[0:1, :]
            slot = jnp.where(first > 0.5, rank, -1.0).astype(jnp.int32)
            top = (lax.broadcasted_iota(jnp.int32, (HB, B), 0) == slot).astype(F32).astype(BF16)
            partner = (lax.broadcasted_iota(jnp.int32, (B, B), 0) == pair).astype(F32).astype(BF16)
            perm[0:HB, :] = top
            perm[HB:B, :] = dot(top, partner).astype(BF16)
            ep[...] = dot(perm[...], emb_v[...]).astype(BF16)
            uz, _ = unit(ep[...].astype(F32))
            zall[0, ic] = uz.astype(BF16)

        def scores(h, js):
            rows = pl.ds(pl.multiple_of(h * B, B), B)
            zb = zall[0, h]
            for j in js:
                cols = slice(j * 256, (j + 1) * 256)
                e = jnp.exp(dot(zb, chat[cols, :], NT) * 10.0)
                K[rows, cols] = e * e
                part = dot(e.astype(BF16), chat[cols, :])
                P1[h] = part if j == 0 else P1[h] + part
                two = e[:, :128] + e[:, 128:]
                racc[rows, :] = two if j == 0 else racc[rows, :] + two

        def col_send(t):
            if t:
                for j in range(CC):
                    crow[j : j + 1, :] = jnp.sum(colacc[:, j * 128 : (j + 1) * 128], axis=0, keepdims=True)
            csend[t] = crow[...].astype(BF16)
            for i, o in enumerate(XZ):
                send(csend.at[t], crecv.at[t, i + 1], cs.at[t], cr.at[t], o)
            pltpu.make_async_copy(csend.at[t], crecv.at[t, 0], cr.at[t]).start()

        def col_take(t):
            take(crecv.at[t], cr.at[t])
            crow[...] = 1.0 / jnp.sum(crecv[t].astype(F32), axis=0)

        def row_pass(out, blocks):
            for i in range(blocks[0] * BC, (blocks[-1] + 1) * BC):
                rows = slice(i * 128, (i + 1) * 128)
                acc = jnp.zeros((128, 128), F32)
                for j in range(CC):
                    acc = acc + K[rows, j * 128 : (j + 1) * 128] * crow[j : j + 1, :]
                out[i // BC, i % BC : i % BC + 1, :] = jnp.sum(acc.T, axis=0, keepdims=True)

        def col_pass(t):
            for blk in range(C):
                take(rrecv.at[t, blk], rr.at[t * C + blk])
                rrow[...] = 1.0 / jnp.sum(rrecv[t, blk], axis=0)
                for i in range(BC):
                    rb[i * 128 : (i + 1) * 128, :] = spread(rrow[i : i + 1, :])

                for jg in range(0, CC, 8):
                    acc = [jnp.zeros((8, 128), F32) for _ in range(8)]
                    for i in range(BC):
                        r = rb[i * 128 : (i + 1) * 128, :]
                        rows = slice(blk * B + i * 128, blk * B + (i + 1) * 128)
                        for j in range(8):
                            p = K[rows, (jg + j) * 128 : (jg + j + 1) * 128] * r
                            acc[j] = acc[j] + jnp.sum(p.reshape(16, 8, 128), axis=0)
                    for j in range(8):
                        cols = slice((jg + j) * 128, (jg + j + 1) * 128)
                        colacc[:, cols] = colacc[:, cols] + acc[j] if blk else acc[j]

        def row_send(t):
            for blk in range(C):
                row_pass(rsend.at[t], (blk,))
                for i, o in enumerate(YC):
                    send(rsend.at[t, blk], rrecv.at[t, blk, i + 1], rs.at[t * C + blk], rr.at[t * C + blk], o)
                pltpu.make_async_copy(rsend.at[t, blk], rrecv.at[t, blk, 0], rr.at[t * C + blk]).start()

        def scores_t(a):
            mine = mine_c[...]
            for c in range(C):
                for q in range(B // 256):
                    n = (a * C + c) * (B // 256)
                    zb = zall[a, c, q * 256 : (q + 1) * 256, :]
                    e = jnp.exp(dot(mine, zb, NT) * 10.0)
                    KT[:, (n + 1 - q) * 256 : (n + 2 - q) * 256] = (e * e).astype(BF16)
                    i = c * BC + q * 2
                    p = [
                        (e[:, h * 128 : (h + 1) * 128] * rp4[a, i + h : i + h + 1, :]).astype(BF16) for h in range(2)
                    ]
                    part = dot(jnp.concatenate(p, axis=1), zb)
                    TP[...] = part if a + c + q == 0 else TP[...] + part

        def send_x(a):
            send(zall.at[0, ic], zall.at[a, ic], xs, xr.at[a], (a, 0, 0, 0))

        def forward(a):
            send(zall.at[a, ic], zall.at[a, ic], fs, fr.at[a], (0, 0, 1, 0))

        def relay(a, half):
            rows = pl.ds(half * HB, HB)
            send(zall.at[a, ic, rows], zall.at[FAR, ic, rows], xs, xr.at[FAR], (a, 0, 0, 0))

        take(frecv, f_r)
        crow[...] = crow[...] + frecv[...]
        col_send(0)
        reorder()
        send(zall.at[0, ic], zall.at[0, ic], core_s, core_r, (0, 0, 1, 0))
        for a in NEAR:
            send_x(a)
        scores(ic, range(NC // 256))
        take(zall.at[0, 1 - ic], core_r)
        scores(1 - ic, range(NC // 256))
        send(P1.at[1 - ic], precv, p_s, p_r, (0, 0, 1, 0))
        for i in range(RC):
            tsend[i : i + 1, :] = jnp.sum(racc[i * 128 : (i + 1) * 128, :].T, axis=0, keepdims=True)
        for i, o in enumerate(YC):
            send(tsend, trecv.at[i + 1], ts, tr, o)
        pltpu.make_async_copy(tsend, trecv.at[0], tr).start()
        col_take(0)
        row_send(0)
        permt[...] = perm[...].astype(F32).T.astype(BF16)
        for k, b in enumerate(FZ):
            mine_c[k * OB : (k + 1) * OB, :] = chat[pl.ds(pl.multiple_of(ix * TC + (iz + b) % Z * OB, OB), OB), :]
        take(trecv, tr)
        rp4[0] = 10.0 / jnp.sum(trecv[...], axis=0)
        for a in range(1, X):
            send(rp4.at[0], rp4.at[a], ps, pr.at[a], (a, 0, 0, 0))

        col_pass(0)
        col_send(1)
        take(precv, p_r)
        for i in range(BC):
            rows = slice(i * 128, (i + 1) * 128)
            rp = spread(rp4[0, pl.ds(ic * BC + i, 1), :])
            pown[rows, :] = (P1[ic, rows, :] + precv[rows, :]) * jnp.concatenate([rp, rp], axis=1)
        scores_t(0)
        for half, a in enumerate(NEAR):
            take(zall.at[a, ic], xr.at[a])
            relay(a, half)
        for a in NEAR:
            forward(a)
        col_take(1)
        row_send(1)
        for a in NEAR:
            take(rp4.at[a], pr.at[a])
            take(zall.at[a, 1 - ic], fr.at[a])
            scores_t(a)

        col_pass(1)
        col_send(2)
        take(zall.at[FAR, ic], xr.at[FAR])
        forward(FAR)
        take(rp4.at[FAR], pr.at[FAR])
        take(zall.at[FAR, 1 - ic], fr.at[FAR])
        scores_t(FAR)
        col_take(2)
        row_pass(rsend3, range(C))
        for o in sorted(XYC, key=lambda o: o[0] != 0):
            send(rsend3, rrecv3.at[o[0] * GR + YCI[(0,) + o[1:]]], rs.at[4], rr.at[5 if o[0] else 4], o)
        pltpu.make_async_copy(rsend3, rrecv3.at[0], rr.at[4]).start()
        def codes(h):
            for q in range(2):
                rows = pl.ds(pl.multiple_of(h * B + q * HB, HB), HB)
                w = [(K[rows, j * 128 : (j + 1) * 128] * crow[j : j + 1, :]).astype(BF16) for j in range(CC)]
                U[h, q] = dot(jnp.concatenate(w, axis=1), chat[...])

        codes(1 - ic)
        send(U.at[1 - ic], urecv, ks, kr, (0, 0, 1, 0))
        codes(ic)
        mine = crow[pl.ds(ix * (TC // 128), TC // 128), :]
        for i in range(TC // 128):
            c3a[i * 128 : (i + 1) * 128, :] = spread(mine[i : i + 1, :])
        for k, b in enumerate(FZ):
            c3b[k * OB : (k + 1) * OB, :] = c3a[pl.ds(pl.multiple_of((iz + b) % Z * OB, OB), OB), :]
        take(urecv, kr)
        U[ic] = U[ic] + urecv[...]
        take(rrecv3.at[pl.ds(0, GR)], rr.at[4])
        r34[0] = 10.0 / jnp.sum(rrecv3[0:GR], axis=0).reshape(RC, 128)
        for i in range(BC):
            q, rows = i * 128 // HB, slice(i * 128 % HB, i * 128 % HB + 128)
            r3 = spread(r34[0, pl.ds(ic * BC + i, 1), :])
            mine = pown[(1 - q) * HB + i * 128 % HB : (1 - q) * HB + i * 128 % HB + 128, :]
            gpart[1 - q, rows, :] = mine - U[ic, q, rows, :] * jnp.concatenate([r3, r3], axis=1)
        far_y = sorted(range(1, Y), key=lambda k: -ring(k, Y))
        for q in range(2):
            ysend[q] = gpart[q].reshape(Y, HB // Y, D).astype(BF16)
            for f in far_y:
                send(ysend.at[q, (iy + f) % Y], yrecv.at[q, f - 1], ys.at[q], yr.at[q], (0, 0, 0, f))

        take(rrecv3.at[pl.ds(GR, (X - 1) * GR)], rr.at[5])
        for a in range(1, X):
            r34[a] = 10.0 / jnp.sum(rrecv3[a * GR : (a + 1) * GR], axis=0).reshape(RC, 128)
        HT, ZH = TC // 2, Z // 2

        def grad_t(m, _):
            rows = pl.ds(pl.multiple_of(m * HT, HT), HT)
            g = []
            for n in range(X * RC):
                a, q = n // RC, n % RC
                qp = q // BC * BC + (q + BC // 2) % BC
                g.append(KT[rows, n * 128 : (n + 1) * 128] * r34[a, qp : qp + 1, :].astype(BF16))
            part = dot(jnp.concatenate(g, axis=1), zall[...].reshape(X * RT, D))
            c3 = c3b[rows, :]
            part = TP[rows, :] - part * jnp.concatenate([c3, c3], axis=1)
            tpart[rows, :] = part
            zsend[pl.ds(m * ZH, ZH)] = part.reshape(ZH, OB, D).astype(BF16)
            for k in range(ZH):
                b = Z // 2 + m * (ZH // 2) + k // 2 if k % 2 == 0 else Z // 2 - m * (ZH // 2) - (k + 1) // 2
                to = {"dp": (ix * Z + (iz + b) % Z) * C + ic, "proto": iy}

                def go(k=k, to=to):
                    pltpu.make_async_remote_copy(
                        src_ref=zsend.at[m * ZH + k], dst_ref=zrecv.at[m * ZH + k], send_sem=zs, recv_sem=zr,
                        device_id=to, device_id_type=MESH,
                    ).start()

                if k < ZH - 1:
                    go()
                else:
                    pl.when(m == 0)(go)
            return 0

        lax.fori_loop(0, 2, grad_t, 0)

        SB = HB // Y
        for q in range(2):
            take(yrecv.at[q], yr.at[q])
            at = pl.ds(pl.multiple_of(iy * SB, SB), SB)
            gzs = gpart[q, at, :] + jnp.sum(yrecv[q].astype(F32), axis=0)
            uq, nq = unit(ep[pl.ds(pl.multiple_of(q * HB + iy * SB, SB), SB), :].astype(F32))
            yall[q, iy] = ((gzs - uq * jnp.sum(uq * gzs, axis=1, keepdims=True)) / nq).astype(BF16)
            for f in far_y:
                send(yall.at[q, iy], yall.at[q, iy], gs.at[q], gr.at[q], (0, 0, 0, f))

        take(zrecv, zr)
        gcs = tpart[(Z - 1) * OB : Z * OB, :] + jnp.sum(zrecv[...].astype(F32), axis=0)
        uc, nc = unit(praw[0, ix * Z + iz].astype(F32))
        gc_ref[...] = (gcs - uc * jnp.sum(uc * gcs, axis=1, keepdims=True)) / nc
        for q in range(2):
            take(yall.at[q, pl.ds(0, Y - 1)], gr.at[q])
        gz_ref[...] = dot(permt[...], yall[...].reshape(B, D))

        take(zall.at[0, ic], core_s)
        take(zall.at[pl.ds(0, X - 1), 0], xs)
        take(zall.at[pl.ds(0, X - 1), 0], fs)
        take(rp4.at[pl.ds(0, X - 1)], ps)
        for t in range(3):
            take(crecv.at[t, pl.ds(0, len(XZ))], cs.at[t])
        take(fsend, f_s)
        take(precv, p_s)
        take(urecv, ks)
        take(trecv.at[pl.ds(0, len(YC))], ts)
        for t in range(2):
            for blk in range(C):
                take(rrecv.at[t, blk, pl.ds(0, len(YC))], rs.at[t * C + blk])
        take(rrecv3.at[pl.ds(0, len(XYC))], rs.at[4])
        take(zrecv, zs)
        for q in range(2):
            take(yrecv.at[q], ys.at[q])
            take(yall.at[q, pl.ds(0, Y - 1)], gs.at[q])

    V = pltpu.VMEM
    S = pltpu.SemaphoreType.DMA
    scratch = [
        V((1, B), jnp.int32),
        V((B, D), BF16),
        V((B, D), BF16),
        V((C, X * Z, OB, D), BF16),
        V((NC, D), BF16),
        V((NC, D), BF16),
        V((B, D), BF16),
        V((B, B), BF16),
        V((B, B), BF16),
        V((X, C, B, D), BF16),
        V((RT, NC), F32),
        V((TC, X * RT), BF16),
        V((C, B, D), F32),
        V((B, D), F32),
        V((B, D), F32),
        V((TC, D), F32),
        V((C, 2, HB, D), F32),
        V((2, HB, D), F32),
        V((8, NC), F32),
        V((RT, 128), F32),
        V((B, 128), F32),
        V((TC, 128), F32),
        V((TC, 128), F32),
        V((TC, D), BF16),
        V((CC, 128), F32),
        V((BC, 128), F32),
        V((X, RC, 128), F32),
        V((X, RC, 128), F32),
        V((3, CC, 128), BF16),
        V((3, len(XZ) + 1, CC, 128), BF16),
        V((CC, 128), F32),
        V((CC, 128), F32),
        V((RC, 128), F32),
        V((GR, RC, 128), F32),
        V((2, C, BC, 128), F32),
        V((2, C, GR, BC, 128), F32),
        V((C, BC, 128), F32),
        V((X * GR, C, BC, 128), F32),
        V((2, HB, D), F32),
        V((TC, D), F32),
        V((Z, OB, D), BF16),
        V((Z - 1, OB, D), BF16),
        V((2, Y, HB // Y, D), BF16),
        V((2, Y - 1, HB // Y, D), BF16),
        V((2, Y, HB // Y, D), BF16),
        S((4,)),
        S, S,
        S, S((X,)),
        S, S((X,)),
        S((3,)), S((3,)),
        S, S,
        S, S,
        S((5,)), S((6,)),
        S, S((X,)),
        S, S,
        S, S,
        S, S,
        S((2,)), S((2,)),
        S((2,)), S((2,)),
    ]
    return kernel, scratch


def place(gz_ref, gc_ref, gz_out, gc_out, sem):
    copies = [
        pltpu.make_async_copy(gz_ref, gz_out, sem.at[0]),
        pltpu.make_async_copy(gc_ref, gc_out, sem.at[1]),
    ]
    for copy in copies:
        copy.start()
    for copy in copies:
        copy.wait()


def body(embeddings, prototypes, pair_index):
    B, D = embeddings.shape
    NCL = prototypes.shape[0]
    NC = NCL // C
    OB = NCL // (X * Z * C)
    kernel, scratch = make_kernel(B, D, NC)
    vm = pl.BlockSpec(memory_space=pltpu.VMEM)
    hbm = pl.BlockSpec(memory_space=pl.ANY)
    shapes = (jax.ShapeDtypeStruct((B, D), F32), jax.ShapeDtypeStruct((OB, D), F32))
    held = (pltpu.VMEM((B, D), F32), pltpu.VMEM((OB, D), F32))
    grads = pl.pallas_call(
        kernel,
        out_shape=held,
        in_specs=[hbm, hbm, hbm],
        out_specs=(vm, vm),
        scratch_shapes=scratch,
        compiler_params=pltpu.CompilerParams(
            collective_id=0, has_side_effects=True, vmem_limit_bytes=60 * 2**20
        ),
        name="swav",
    )(embeddings, prototypes.reshape(X * Z, C, OB, D), pair_index.reshape(1, B))
    return pl.pallas_call(
        place,
        out_shape=shapes,
        in_specs=[vm, vm],
        out_specs=(hbm, hbm),
        scratch_shapes=[pltpu.SemaphoreType.DMA((2,))],
        name="place",
    )(*(pltpu.with_memory_space_constraint(g, pltpu.VMEM) for g in grads))


def solution(mesh):
    return jax.shard_map(
        body,
        mesh=mesh,
        in_specs=(P("dp", None), P("proto", None), P("dp")),
        out_specs=(P("dp", None), P(("proto", "dp"), None)),
        check_vma=False,
    )
```

```python
import jax
import jax.numpy as jnp
from jax import lax
from jax.experimental import pallas as pl
from jax.experimental.pallas import tpu as pltpu
from jax.sharding import PartitionSpec as P

X, Z, C, Y = 4, 8, 2, 4
MESH = pl.DeviceIdType.MESH
F32, BF16 = jnp.float32, jnp.bfloat16
NT = (((1,), (1,)), ((), ()))
NN = (((1,), (0,)), ((), ()))


def ring(k, n):
    return min(k, n - k)


def offsets(axes):
    span = [n if a in axes else 1 for a, n in zip("xzcy", (X, Z, C, Y))]
    out = [
        (a, b, e, f)
        for a in range(span[0])
        for b in range(span[1])
        for e in range(span[2])
        for f in range(span[3])
        if a or b or e or f
    ]
    return sorted(out, key=farthest)


def farthest(t):
    return -(4 * (ring(t[0], X) + ring(t[1], Z) + ring(t[3], Y)) + t[2])


def dot(a, b, dims=NN):
    return lax.dot_general(a, b, dims, preferred_element_type=F32)


def unit(values):
    norm = jnp.sqrt(jnp.sum(values * values, axis=1, keepdims=True) + 1e-06)
    return values / norm, norm


def spread(row):
    return jnp.broadcast_to(row, (128, 128)).T


def make_kernel(B, D, NC):
    RT, RC, CC, TC = C * B, C * B // 128, NC // 128, NC // X
    OB = TC // Z
    BC = B // 128
    HB = B // 2
    FZ = [Z // 2 + k // 2 if k % 2 == 0 else Z // 2 - (k + 1) // 2 for k in range(Z)]
    NEAR, FAR = (1, X - 1), 2
    XZ, YC, XYC = offsets("xz"), offsets("yc"), offsets("xyc")

    GR = len(YC) + 1
    YCI = {o: i + 1 for i, o in enumerate(YC)}
    YCI[(0, 0, 0, 0)] = 0

    def kernel(
        emb_ref, proto_ref, pair_ref, gz_ref, gc_ref,
        pair_v, emb_v, zu, praw, chat, chato, ep, perm, permt, zall, K, KT, P1, precv, pown, TP, U, urecv, colacc, racc, rb, c3a, c3b, mine_c,
        crow, rrow, rp4, r34, csend, crecv, fsend, frecv, tsend, trecv, rsend, rrecv, rsend3, rrecv3,
        gpart, tpart, zsend, zrecv, ysend, yrecv, yall,
        lsem, core_s, core_r, xs, xr, fs, fr, cs, cr, f_s, f_r, ts, tr, rs, rr, ps, pr, p_s, p_r, ks, kr, zs, zr, ys, yr, gs, gr,
    ):
        dp = lax.axis_index("dp")
        iy = lax.axis_index("proto")
        ix, iz, ic = dp // (Z * C), (dp // C) % Z, dp % C

        def dev(o):
            a, b, e, f = o
            nx = (ix + a) % X if a else ix
            nz = (iz + b) % Z if b else iz
            nc = (ic + e) % C if e else ic
            ny = (iy + f) % Y if f else iy
            return {"dp": (nx * Z + nz) * C + nc, "proto": ny}

        def send(src, dst, s, r, o):
            pltpu.make_async_remote_copy(
                src_ref=src, dst_ref=dst, send_sem=s, recv_sem=r, device_id=dev(o), device_id_type=MESH
            ).start()

        def take(ref, sem):
            pltpu.make_async_copy(ref, ref, sem).wait()

        loads = [
            pltpu.make_async_copy(pair_ref, pair_v, lsem.at[0]),
            pltpu.make_async_copy(emb_ref, emb_v, lsem.at[1]),
            pltpu.make_async_copy(proto_ref.at[:, 1 - ic], praw.at[1], lsem.at[2]),
            pltpu.make_async_copy(proto_ref.at[:, ic], praw.at[0], lsem.at[3]),
        ]
        for load in loads:
            load.start()
        barrier = pltpu.get_barrier_semaphore()
        everyone = sorted(sorted(set(XZ + YC + XYC)), key=farthest)
        for o in everyone:
            pl.semaphore_signal(barrier, inc=1, device_id=dev(o), device_id_type=MESH)

        loads[1].wait()
        loads[0].wait()
        v = emb_v[...].astype(F32)
        zu[...] = (v * (1.0 / jnp.sqrt(jnp.sum(v * v, axis=1, keepdims=True) + 1e-06))).astype(BF16)
        NB = 256 // OB

        def norm_c(half, out):
            def step(i, _):
                v = praw[half, pl.ds(i * NB, NB)].reshape(256, D).astype(F32)
                inv = 1.0 / jnp.sqrt(jnp.sum(v * v, axis=1, keepdims=True) + 1e-06)
                out[pl.ds(pl.multiple_of(i * 256, 256), 256), :] = (v * inv).astype(BF16)
                return 0

            lax.fori_loop(0, NC // 256, step, 0, unroll=2)

        def first_totals(prototypes, out):
            zb = zu[...]
            for j in range(NC // 256):
                k = jnp.exp(dot(zb, prototypes[j * 256 : (j + 1) * 256, :], NT) * 20.0)
                colacc[:, j * 256 : (j + 1) * 256] = jnp.sum(k.reshape(B // 8, 8, 256), axis=0)
            for j in range(CC):
                out[j : j + 1, :] = jnp.sum(colacc[:, j * 128 : (j + 1) * 128], axis=0, keepdims=True)

        loads[2].wait()
        norm_c(1, chato)
        first_totals(chato, fsend)
        loads[3].wait()
        norm_c(0, chat)
        pl.semaphore_wait(barrier, len(everyone))
        send(fsend, frecv, f_s, f_r, (0, 0, 1, 0))
        first_totals(chat, crow)

        def reorder():
            pair = pair_v[...]
            lane = lax.broadcasted_iota(jnp.int32, (1, B), 1)
            first = (lane < pair).astype(F32)
            up = (
                lax.broadcasted_iota(jnp.int32, (B, B), 0) < lax.broadcasted_iota(jnp.int32, (B, B), 1)
            ).astype(F32).astype(BF16)
            rank = dot(jnp.broadcast_to(first, (8, B)).astype(BF16), up)[0:1, :]
            slot = jnp.where(first > 0.5, rank, -1.0).astype(jnp.int32)
            top = (lax.broadcasted_iota(jnp.int32, (HB, B), 0) == slot).astype(F32).astype(BF16)
            partner = (lax.broadcasted_iota(jnp.int32, (B, B), 0) == pair).astype(F32).astype(BF16)
            perm[0:HB, :] = top
            perm[HB:B, :] = dot(top, partner).astype(BF16)
            ep[...] = dot(perm[...], emb_v[...]).astype(BF16)
            uz, _ = unit(ep[...].astype(F32))
            zall[0, ic] = uz.astype(BF16)

        def scores(h, js):
            rows = pl.ds(pl.multiple_of(h * B, B), B)
            zb = zall[0, h]
            for j in js:
                cols = slice(j * 256, (j + 1) * 256)
                e = jnp.exp(dot(zb, chat[cols, :], NT) * 10.0)
                K[rows, cols] = e * e
                part = dot(e.astype(BF16), chat[cols, :])
                P1[h] = part if j == 0 else P1[h] + part
                two = e[:, :128] + e[:, 128:]
                racc[rows, :] = two if j == 0 else racc[rows, :] + two

        def col_send(t):
            if t:
                for j in range(CC):
                    crow[j : j + 1, :] = jnp.sum(colacc[:, j * 128 : (j + 1) * 128], axis=0, keepdims=True)
            csend[t] = crow[...].astype(BF16)
            for i, o in enumerate(XZ):
                send(csend.at[t], crecv.at[t, i + 1], cs.at[t], cr.at[t], o)
            pltpu.make_async_copy(csend.at[t], crecv.at[t, 0], cr.at[t]).start()

        def col_take(t):
            take(crecv.at[t], cr.at[t])
            crow[...] = 1.0 / jnp.sum(crecv[t].astype(F32), axis=0)

        def row_pass(out, blocks):
            for i in range(blocks[0] * BC, (blocks[-1] + 1) * BC):
                rows = slice(i * 128, (i + 1) * 128)
                acc = jnp.zeros((128, 128), F32)
                for j in range(CC):
                    acc = acc + K[rows, j * 128 : (j + 1) * 128] * crow[j : j + 1, :]
                out[i // BC, i % BC : i % BC + 1, :] = jnp.sum(acc.T, axis=0, keepdims=True)

        def col_pass(t):
            for blk in range(C):
                take(rrecv.at[t, blk], rr.at[t * C + blk])
                rrow[...] = 1.0 / jnp.sum(rrecv[t, blk], axis=0)
                for i in range(BC):
                    rb[i * 128 : (i + 1) * 128, :] = spread(rrow[i : i + 1, :])

                for jg in range(0, CC, 8):
                    acc = [jnp.zeros((8, 128), F32) for _ in range(8)]
                    for i in range(BC):
                        r = rb[i * 128 : (i + 1) * 128, :]
                        rows = slice(blk * B + i * 128, blk * B + (i + 1) * 128)
                        for j in range(8):
                            p = K[rows, (jg + j) * 128 : (jg + j + 1) * 128] * r
                            acc[j] = acc[j] + jnp.sum(p.reshape(16, 8, 128), axis=0)
                    for j in range(8):
                        cols = slice((jg + j) * 128, (jg + j + 1) * 128)
                        colacc[:, cols] = colacc[:, cols] + acc[j] if blk else acc[j]

        def row_send(t):
            for blk in range(C):
                row_pass(rsend.at[t], (blk,))
                for i, o in enumerate(YC):
                    send(rsend.at[t, blk], rrecv.at[t, blk, i + 1], rs.at[t * C + blk], rr.at[t * C + blk], o)
                pltpu.make_async_copy(rsend.at[t, blk], rrecv.at[t, blk, 0], rr.at[t * C + blk]).start()

        def scores_t(a):
            mine = mine_c[...]
            for c in range(C):
                for q in range(B // 256):
                    n = (a * C + c) * (B // 256)
                    zb = zall[a, c, q * 256 : (q + 1) * 256, :]
                    e = jnp.exp(dot(mine, zb, NT) * 10.0)
                    KT[:, (n + 1 - q) * 256 : (n + 2 - q) * 256] = (e * e).astype(BF16)
                    i = c * BC + q * 2
                    p = [
                        (e[:, h * 128 : (h + 1) * 128] * rp4[a, i + h : i + h + 1, :]).astype(BF16) for h in range(2)
                    ]
                    part = dot(jnp.concatenate(p, axis=1), zb)
                    TP[...] = part if a + c + q == 0 else TP[...] + part

        def send_x(a):
            send(zall.at[0, ic], zall.at[a, ic], xs, xr.at[a], (a, 0, 0, 0))

        def forward(a):
            send(zall.at[a, ic], zall.at[a, ic], fs, fr.at[a], (0, 0, 1, 0))

        def relay(a, half):
            rows = pl.ds(half * HB, HB)
            send(zall.at[a, ic, rows], zall.at[FAR, ic, rows], xs, xr.at[FAR], (a, 0, 0, 0))

        take(frecv, f_r)
        crow[...] = crow[...] + frecv[...]
        col_send(0)
        reorder()
        send(zall.at[0, ic], zall.at[0, ic], core_s, core_r, (0, 0, 1, 0))
        for a in NEAR:
            send_x(a)
        scores(ic, range(NC // 256))
        take(zall.at[0, 1 - ic], core_r)
        scores(1 - ic, range(NC // 256))
        send(P1.at[1 - ic], precv, p_s, p_r, (0, 0, 1, 0))
        for i in range(RC):
            tsend[i : i + 1, :] = jnp.sum(racc[i * 128 : (i + 1) * 128, :].T, axis=0, keepdims=True)
        for i, o in enumerate(YC):
            send(tsend, trecv.at[i + 1], ts, tr, o)
        pltpu.make_async_copy(tsend, trecv.at[0], tr).start()
        col_take(0)
        row_send(0)
        permt[...] = perm[...].astype(F32).T.astype(BF16)
        for k, b in enumerate(FZ):
            mine_c[k * OB : (k + 1) * OB, :] = chat[pl.ds(pl.multiple_of(ix * TC + (iz + b) % Z * OB, OB), OB), :]
        take(trecv, tr)
        rp4[0] = 10.0 / jnp.sum(trecv[...], axis=0)
        for a in range(1, X):
            send(rp4.at[0], rp4.at[a], ps, pr.at[a], (a, 0, 0, 0))

        col_pass(0)
        col_send(1)
        take(precv, p_r)
        for i in range(BC):
            rows = slice(i * 128, (i + 1) * 128)
            rp = spread(rp4[0, pl.ds(ic * BC + i, 1), :])
            pown[rows, :] = (P1[ic, rows, :] + precv[rows, :]) * jnp.concatenate([rp, rp], axis=1)
        scores_t(0)
        for half, a in enumerate(NEAR):
            take(zall.at[a, ic], xr.at[a])
            relay(a, half)
        for a in NEAR:
            forward(a)
        col_take(1)
        row_send(1)
        for a in NEAR:
            take(rp4.at[a], pr.at[a])
            take(zall.at[a, 1 - ic], fr.at[a])
            scores_t(a)

        col_pass(1)
        col_send(2)
        take(zall.at[FAR, ic], xr.at[FAR])
        forward(FAR)
        take(rp4.at[FAR], pr.at[FAR])
        take(zall.at[FAR, 1 - ic], fr.at[FAR])
        scores_t(FAR)
        col_take(2)
        row_pass(rsend3, range(C))
        for o in sorted(XYC, key=lambda o: o[0] != 0):
            send(rsend3, rrecv3.at[o[0] * GR + YCI[(0,) + o[1:]]], rs.at[4], rr.at[5 if o[0] else 4], o)
        pltpu.make_async_copy(rsend3, rrecv3.at[0], rr.at[4]).start()
        def codes(h):
            for q in range(2):
                rows = pl.ds(pl.multiple_of(h * B + q * HB, HB), HB)
                w = [(K[rows, j * 128 : (j + 1) * 128] * crow[j : j + 1, :]).astype(BF16) for j in range(CC)]
                U[h, q] = dot(jnp.concatenate(w, axis=1), chat[...])

        codes(1 - ic)
        send(U.at[1 - ic], urecv, ks, kr, (0, 0, 1, 0))
        codes(ic)
        mine = crow[pl.ds(ix * (TC // 128), TC // 128), :]
        for i in range(TC // 128):
            c3a[i * 128 : (i + 1) * 128, :] = spread(mine[i : i + 1, :])
        for k, b in enumerate(FZ):
            c3b[k * OB : (k + 1) * OB, :] = c3a[pl.ds(pl.multiple_of((iz + b) % Z * OB, OB), OB), :]
        take(urecv, kr)
        U[ic] = U[ic] + urecv[...]
        take(rrecv3.at[pl.ds(0, GR)], rr.at[4])
        r34[0] = 10.0 / jnp.sum(rrecv3[0:GR], axis=0).reshape(RC, 128)
        for i in range(BC):
            q, rows = i * 128 // HB, slice(i * 128 % HB, i * 128 % HB + 128)
            r3 = spread(r34[0, pl.ds(ic * BC + i, 1), :])
            mine = pown[(1 - q) * HB + i * 128 % HB : (1 - q) * HB + i * 128 % HB + 128, :]
            gpart[1 - q, rows, :] = mine - U[ic, q, rows, :] * jnp.concatenate([r3, r3], axis=1)
        far_y = sorted(range(1, Y), key=lambda k: -ring(k, Y))
        for q in range(2):
            ysend[q] = gpart[q].reshape(Y, HB // Y, D).astype(BF16)
            for f in far_y:
                send(ysend.at[q, (iy + f) % Y], yrecv.at[q, f - 1], ys.at[q], yr.at[q], (0, 0, 0, f))

        def codes_t(rows, sources):
            g = []
            for n in range(sources[0] * RC, (sources[-1] + 1) * RC):
                a, q = n // RC, n % RC
                qp = q // BC * BC + (q + BC // 2) % BC
                g.append(KT[rows, n * 128 : (n + 1) * 128] * r34[a, qp : qp + 1, :].astype(BF16))
            zb = zall[sources[0] : sources[-1] + 1].reshape(len(sources) * RT, D)
            return dot(jnp.concatenate(g, axis=1), zb)

        tpart[...] = codes_t(slice(0, TC), (0,))
        take(rrecv3.at[pl.ds(GR, (X - 1) * GR)], rr.at[5])
        for a in range(1, X):
            r34[a] = 10.0 / jnp.sum(rrecv3[a * GR : (a + 1) * GR], axis=0).reshape(RC, 128)
        HT, ZH = TC // 2, Z // 2

        def grad_t(m, _):
            rows = pl.ds(pl.multiple_of(m * HT, HT), HT)
            part = tpart[rows, :] + codes_t(rows, range(1, X))
            c3 = c3b[rows, :]
            part = TP[rows, :] - part * jnp.concatenate([c3, c3], axis=1)
            tpart[rows, :] = part
            zsend[pl.ds(m * ZH, ZH)] = part.reshape(ZH, OB, D).astype(BF16)
            for k in range(ZH):
                b = Z // 2 + m * (ZH // 2) + k // 2 if k % 2 == 0 else Z // 2 - m * (ZH // 2) - (k + 1) // 2
                to = {"dp": (ix * Z + (iz + b) % Z) * C + ic, "proto": iy}

                def go(k=k, to=to):
                    pltpu.make_async_remote_copy(
                        src_ref=zsend.at[m * ZH + k], dst_ref=zrecv.at[m * ZH + k], send_sem=zs, recv_sem=zr,
                        device_id=to, device_id_type=MESH,
                    ).start()

                if k < ZH - 1:
                    go()
                else:
                    pl.when(m == 0)(go)
            return 0

        lax.fori_loop(0, 2, grad_t, 0)

        SB = HB // Y
        uc, nc = unit(praw[0, ix * Z + iz].astype(F32))
        units = [unit(ep[pl.ds(pl.multiple_of(q * HB + iy * SB, SB), SB), :].astype(F32)) for q in range(2)]
        for q in range(2):
            uq, nq = units[q]
            take(yrecv.at[q], yr.at[q])
            at = pl.ds(pl.multiple_of(iy * SB, SB), SB)
            gzs = gpart[q, at, :] + jnp.sum(yrecv[q].astype(F32), axis=0)
            yall[q, iy] = ((gzs - uq * jnp.sum(uq * gzs, axis=1, keepdims=True)) / nq).astype(BF16)
            for f in far_y:
                send(yall.at[q, iy], yall.at[q, iy], gs.at[q], gr.at[q], (0, 0, 0, f))

        for q in range(2):
            take(yall.at[q, pl.ds(0, Y - 1)], gr.at[q])
        gz_ref[...] = dot(permt[...], yall[...].reshape(B, D))
        take(zrecv, zr)
        gcs = tpart[(Z - 1) * OB : Z * OB, :] + jnp.sum(zrecv[...].astype(F32), axis=0)
        gc_ref[...] = (gcs - uc * jnp.sum(uc * gcs, axis=1, keepdims=True)) / nc

        take(zall.at[0, ic], core_s)
        take(zall.at[pl.ds(0, X - 1), 0], xs)
        take(zall.at[pl.ds(0, X - 1), 0], fs)
        take(rp4.at[pl.ds(0, X - 1)], ps)
        for t in range(3):
            take(crecv.at[t, pl.ds(0, len(XZ))], cs.at[t])
        take(fsend, f_s)
        take(precv, p_s)
        take(urecv, ks)
        take(trecv.at[pl.ds(0, len(YC))], ts)
        for t in range(2):
            for blk in range(C):
                take(rrecv.at[t, blk, pl.ds(0, len(YC))], rs.at[t * C + blk])
        take(rrecv3.at[pl.ds(0, len(XYC))], rs.at[4])
        take(zrecv, zs)
        for q in range(2):
            take(yrecv.at[q], ys.at[q])
            take(yall.at[q, pl.ds(0, Y - 1)], gs.at[q])

    V = pltpu.VMEM
    S = pltpu.SemaphoreType.DMA
    scratch = [
        V((1, B), jnp.int32),
        V((B, D), BF16),
        V((B, D), BF16),
        V((C, X * Z, OB, D), BF16),
        V((NC, D), BF16),
        V((NC, D), BF16),
        V((B, D), BF16),
        V((B, B), BF16),
        V((B, B), BF16),
        V((X, C, B, D), BF16),
        V((RT, NC), F32),
        V((TC, X * RT), BF16),
        V((C, B, D), F32),
        V((B, D), F32),
        V((B, D), F32),
        V((TC, D), F32),
        V((C, 2, HB, D), F32),
        V((2, HB, D), F32),
        V((8, NC), F32),
        V((RT, 128), F32),
        V((B, 128), F32),
        V((TC, 128), F32),
        V((TC, 128), F32),
        V((TC, D), BF16),
        V((CC, 128), F32),
        V((BC, 128), F32),
        V((X, RC, 128), F32),
        V((X, RC, 128), F32),
        V((3, CC, 128), BF16),
        V((3, len(XZ) + 1, CC, 128), BF16),
        V((CC, 128), F32),
        V((CC, 128), F32),
        V((RC, 128), F32),
        V((GR, RC, 128), F32),
        V((2, C, BC, 128), F32),
        V((2, C, GR, BC, 128), F32),
        V((C, BC, 128), F32),
        V((X * GR, C, BC, 128), F32),
        V((2, HB, D), F32),
        V((TC, D), F32),
        V((Z, OB, D), BF16),
        V((Z - 1, OB, D), BF16),
        V((2, Y, HB // Y, D), BF16),
        V((2, Y - 1, HB // Y, D), BF16),
        V((2, Y, HB // Y, D), BF16),
        S((4,)),
        S, S,
        S, S((X,)),
        S, S((X,)),
        S((3,)), S((3,)),
        S, S,
        S, S,
        S((5,)), S((6,)),
        S, S((X,)),
        S, S,
        S, S,
        S, S,
        S((2,)), S((2,)),
        S((2,)), S((2,)),
    ]
    return kernel, scratch


def place(gz_ref, gc_ref, gz_out, gc_out, sem):
    step = gz_ref.shape[0] // 4
    copies = [pltpu.make_async_copy(gc_ref, gc_out, sem.at[4])]
    for i in range(4):
        rows = pl.ds(i * step, step)
        copies.append(pltpu.make_async_copy(gz_ref.at[rows], gz_out.at[rows], sem.at[i]))
    for copy in copies:
        copy.start()
    for copy in copies:
        copy.wait()


def body(embeddings, prototypes, pair_index):
    B, D = embeddings.shape
    NCL = prototypes.shape[0]
    NC = NCL // C
    OB = NCL // (X * Z * C)
    kernel, scratch = make_kernel(B, D, NC)
    vm = pl.BlockSpec(memory_space=pltpu.VMEM)
    hbm = pl.BlockSpec(memory_space=pl.ANY)
    shapes = (jax.ShapeDtypeStruct((B, D), F32), jax.ShapeDtypeStruct((OB, D), F32))
    held = (pltpu.VMEM((B, D), F32), pltpu.VMEM((OB, D), F32))
    grads = pl.pallas_call(
        kernel,
        out_shape=held,
        in_specs=[hbm, hbm, hbm],
        out_specs=(vm, vm),
        scratch_shapes=scratch,
        compiler_params=pltpu.CompilerParams(
            collective_id=0, has_side_effects=True, vmem_limit_bytes=60 * 2**20
        ),
        name="swav",
    )(embeddings, prototypes.reshape(X * Z, C, OB, D), pair_index.reshape(1, B))
    return pl.pallas_call(
        place,
        out_shape=shapes,
        in_specs=[vm, vm],
        out_specs=(hbm, hbm),
        scratch_shapes=[pltpu.SemaphoreType.DMA((5,))],
        name="place",
    )(*(pltpu.with_memory_space_constraint(g, pltpu.VMEM) for g in grads))


def solution(mesh):
    return jax.shard_map(
        body,
        mesh=mesh,
        in_specs=(P("dp", None), P("proto", None), P("dp")),
        out_specs=(P("dp", None), P(("proto", "dp"), None)),
        check_vma=False,
    )
```

```python
import jax
import jax.numpy as jnp
from jax import lax
from jax.experimental import pallas as pl
from jax.experimental.pallas import tpu as pltpu
from jax.sharding import PartitionSpec as P

X, Z, C, Y = 4, 8, 2, 4
MESH = pl.DeviceIdType.MESH
F32, BF16 = jnp.float32, jnp.bfloat16
NT = (((1,), (1,)), ((), ()))
NN = (((1,), (0,)), ((), ()))


def ring(k, n):
    return min(k, n - k)


def offsets(axes):
    span = [n if a in axes else 1 for a, n in zip("xzcy", (X, Z, C, Y))]
    out = [
        (a, b, e, f)
        for a in range(span[0])
        for b in range(span[1])
        for e in range(span[2])
        for f in range(span[3])
        if a or b or e or f
    ]
    return sorted(out, key=farthest)


def farthest(t):
    return -(4 * (ring(t[0], X) + ring(t[1], Z) + ring(t[3], Y)) + t[2])


def dot(a, b, dims=NN):
    return lax.dot_general(a, b, dims, preferred_element_type=F32)


def unit(values):
    norm = jnp.sqrt(jnp.sum(values * values, axis=1, keepdims=True) + 1e-06)
    return values / norm, norm


def spread(row):
    return jnp.broadcast_to(row, (128, 128)).T


def make_kernel(B, D, NC):
    RT, RC, CC, TC = C * B, C * B // 128, NC // 128, NC // X
    OB = TC // Z
    BC = B // 128
    HB = B // 2
    FZ = [Z // 2 + k // 2 if k % 2 == 0 else Z // 2 - (k + 1) // 2 for k in range(Z)]
    NEAR, FAR = (1, X - 1), 2
    XZ, YC, XYC = offsets("xz"), offsets("yc"), offsets("xyc")

    GR = len(YC) + 1
    YCI = {o: i + 1 for i, o in enumerate(YC)}
    YCI[(0, 0, 0, 0)] = 0

    def kernel(
        emb_ref, proto_ref, pair_ref, gz_ref, gc_ref,
        pair_v, emb_v, zu, praw, chat, chato, ep, perm, permt, zall, K, KT, P1, precv, pown, TP, U, urecv, colacc, racc, rb, c3a, c3b, mine_c,
        crow, rrow, rp4, r34, csend, crecv, fsend, frecv, tsend, trecv, rsend, rrecv, rsend3, rrecv3,
        gpart, tpart, zsend, zrecv, ysend, yrecv, yall,
        lsem, core_s, core_r, xs, xr, fs, fr, cs, cr, f_s, f_r, ts, tr, rs, rr, ps, pr, p_s, p_r, ks, kr, zs, zr, ys, yr, gs, gr,
    ):
        dp = lax.axis_index("dp")
        iy = lax.axis_index("proto")
        ix, iz, ic = dp // (Z * C), (dp // C) % Z, dp % C

        def dev(o):
            a, b, e, f = o
            nx = (ix + a) % X if a else ix
            nz = (iz + b) % Z if b else iz
            nc = (ic + e) % C if e else ic
            ny = (iy + f) % Y if f else iy
            return {"dp": (nx * Z + nz) * C + nc, "proto": ny}

        def send(src, dst, s, r, o):
            pltpu.make_async_remote_copy(
                src_ref=src, dst_ref=dst, send_sem=s, recv_sem=r, device_id=dev(o), device_id_type=MESH
            ).start()

        def take(ref, sem):
            pltpu.make_async_copy(ref, ref, sem).wait()

        loads = [
            pltpu.make_async_copy(pair_ref, pair_v, lsem.at[0]),
            pltpu.make_async_copy(emb_ref, emb_v, lsem.at[1]),
            pltpu.make_async_copy(proto_ref.at[:, 1 - ic], praw.at[1], lsem.at[2]),
            pltpu.make_async_copy(proto_ref.at[:, ic], praw.at[0], lsem.at[3]),
        ]
        for load in loads:
            load.start()
        barrier = pltpu.get_barrier_semaphore()
        everyone = sorted(sorted(set(XZ + YC + XYC)), key=farthest)
        for o in everyone:
            pl.semaphore_signal(barrier, inc=1, device_id=dev(o), device_id_type=MESH)

        loads[1].wait()
        loads[0].wait()
        v = emb_v[...].astype(F32)
        zu[...] = (v * (1.0 / jnp.sqrt(jnp.sum(v * v, axis=1, keepdims=True) + 1e-06))).astype(BF16)
        NB = 256 // OB

        def norm_c(half, out):
            def step(i, _):
                v = praw[half, pl.ds(i * NB, NB)].reshape(256, D).astype(F32)
                inv = 1.0 / jnp.sqrt(jnp.sum(v * v, axis=1, keepdims=True) + 1e-06)
                out[pl.ds(pl.multiple_of(i * 256, 256), 256), :] = (v * inv).astype(BF16)
                return 0

            lax.fori_loop(0, NC // 256, step, 0, unroll=2)

        def first_totals(prototypes, out):
            zb = zu[...]
            for j in range(NC // 256):
                k = jnp.exp(dot(zb, prototypes[j * 256 : (j + 1) * 256, :], NT) * 20.0)
                colacc[:, j * 256 : (j + 1) * 256] = jnp.sum(k.reshape(B // 8, 8, 256), axis=0)
            for j in range(CC):
                out[j : j + 1, :] = jnp.sum(colacc[:, j * 128 : (j + 1) * 128], axis=0, keepdims=True)

        loads[2].wait()
        norm_c(1, chato)
        first_totals(chato, fsend)
        loads[3].wait()
        norm_c(0, chat)
        pl.semaphore_wait(barrier, len(everyone))
        send(fsend, frecv, f_s, f_r, (0, 0, 1, 0))
        first_totals(chat, crow)

        def reorder():
            pair = pair_v[...]
            lane = lax.broadcasted_iota(jnp.int32, (1, B), 1)
            first = (lane < pair).astype(F32)
            up = (
                lax.broadcasted_iota(jnp.int32, (B, B), 0) < lax.broadcasted_iota(jnp.int32, (B, B), 1)
            ).astype(F32).astype(BF16)
            rank = dot(jnp.broadcast_to(first, (8, B)).astype(BF16), up)[0:1, :]
            slot = jnp.where(first > 0.5, rank, -1.0).astype(jnp.int32)
            top = (lax.broadcasted_iota(jnp.int32, (HB, B), 0) == slot).astype(F32).astype(BF16)
            partner = (lax.broadcasted_iota(jnp.int32, (B, B), 0) == pair).astype(F32).astype(BF16)
            perm[0:HB, :] = top
            perm[HB:B, :] = dot(top, partner).astype(BF16)
            ep[...] = dot(perm[...], emb_v[...]).astype(BF16)
            uz, _ = unit(ep[...].astype(F32))
            zall[0, ic] = uz.astype(BF16)

        def scores(h, js):
            rows = pl.ds(pl.multiple_of(h * B, B), B)
            zb = zall[0, h]
            for j in js:
                cols = slice(j * 256, (j + 1) * 256)
                e = jnp.exp(dot(zb, chat[cols, :], NT) * 10.0)
                K[rows, cols] = e * e
                part = dot(e.astype(BF16), chat[cols, :])
                P1[h] = part if j == 0 else P1[h] + part
                two = e[:, :128] + e[:, 128:]
                racc[rows, :] = two if j == 0 else racc[rows, :] + two

        def col_send(t):
            if t:
                for j in range(CC):
                    crow[j : j + 1, :] = jnp.sum(colacc[:, j * 128 : (j + 1) * 128], axis=0, keepdims=True)
            csend[t] = crow[...].astype(BF16)
            for i, o in enumerate(XZ):
                send(csend.at[t], crecv.at[t, i + 1], cs.at[t], cr.at[t], o)
            pltpu.make_async_copy(csend.at[t], crecv.at[t, 0], cr.at[t]).start()

        def col_take(t):
            take(crecv.at[t], cr.at[t])
            crow[...] = 1.0 / jnp.sum(crecv[t].astype(F32), axis=0)

        def row_pass(out, blocks):
            for i in range(blocks[0] * BC, (blocks[-1] + 1) * BC):
                rows = slice(i * 128, (i + 1) * 128)
                acc = jnp.zeros((128, 128), F32)
                for j in range(CC):
                    acc = acc + K[rows, j * 128 : (j + 1) * 128] * crow[j : j + 1, :]
                out[i // BC, i % BC : i % BC + 1, :] = jnp.sum(acc.T, axis=0, keepdims=True)

        def col_pass(t):
            for blk in range(C):
                take(rrecv.at[t, blk], rr.at[t * C + blk])
                rrow[...] = 1.0 / jnp.sum(rrecv[t, blk], axis=0)
                for i in range(BC):
                    rb[i * 128 : (i + 1) * 128, :] = spread(rrow[i : i + 1, :])

                for jg in range(0, CC, 8):
                    acc = [jnp.zeros((8, 128), F32) for _ in range(8)]
                    for i in range(BC):
                        r = rb[i * 128 : (i + 1) * 128, :]
                        rows = slice(blk * B + i * 128, blk * B + (i + 1) * 128)
                        for j in range(8):
                            p = K[rows, (jg + j) * 128 : (jg + j + 1) * 128] * r
                            acc[j] = acc[j] + jnp.sum(p.reshape(16, 8, 128), axis=0)
                    for j in range(8):
                        cols = slice((jg + j) * 128, (jg + j + 1) * 128)
                        colacc[:, cols] = colacc[:, cols] + acc[j] if blk else acc[j]

        def row_send(t):
            for blk in range(C):
                row_pass(rsend.at[t], (blk,))
                for i, o in enumerate(YC):
                    send(rsend.at[t, blk], rrecv.at[t, blk, i + 1], rs.at[t * C + blk], rr.at[t * C + blk], o)
                pltpu.make_async_copy(rsend.at[t, blk], rrecv.at[t, blk, 0], rr.at[t * C + blk]).start()

        def scores_t(a):
            mine = mine_c[...]
            for c in range(C):
                for q in range(B // 256):
                    n = (a * C + c) * (B // 256)
                    zb = zall[a, c, q * 256 : (q + 1) * 256, :]
                    e = jnp.exp(dot(mine, zb, NT) * 10.0)
                    KT[:, (n + 1 - q) * 256 : (n + 2 - q) * 256] = (e * e).astype(BF16)
                    i = c * BC + q * 2
                    p = [
                        (e[:, h * 128 : (h + 1) * 128] * rp4[a, i + h : i + h + 1, :]).astype(BF16) for h in range(2)
                    ]
                    part = dot(jnp.concatenate(p, axis=1), zb)
                    TP[...] = part if a + c + q == 0 else TP[...] + part

        def send_x(a):
            send(zall.at[0, ic], zall.at[a, ic], xs, xr.at[a], (a, 0, 0, 0))

        def forward(a):
            send(zall.at[a, ic], zall.at[a, ic], fs, fr.at[a], (0, 0, 1, 0))

        def relay(a, half):
            rows = pl.ds(half * HB, HB)
            send(zall.at[a, ic, rows], zall.at[FAR, ic, rows], xs, xr.at[FAR], (a, 0, 0, 0))

        take(frecv, f_r)
        crow[...] = crow[...] + frecv[...]
        col_send(0)
        reorder()
        send(zall.at[0, ic], zall.at[0, ic], core_s, core_r, (0, 0, 1, 0))
        for a in NEAR:
            send_x(a)
        scores(ic, range(NC // 256))
        take(zall.at[0, 1 - ic], core_r)
        scores(1 - ic, range(NC // 256))
        send(P1.at[1 - ic], precv, p_s, p_r, (0, 0, 1, 0))
        for i in range(RC):
            tsend[i : i + 1, :] = jnp.sum(racc[i * 128 : (i + 1) * 128, :].T, axis=0, keepdims=True)
        for i, o in enumerate(YC):
            send(tsend, trecv.at[i + 1], ts, tr, o)
        pltpu.make_async_copy(tsend, trecv.at[0], tr).start()
        col_take(0)
        row_send(0)
        permt[...] = perm[...].astype(F32).T.astype(BF16)
        for k, b in enumerate(FZ):
            mine_c[k * OB : (k + 1) * OB, :] = chat[pl.ds(pl.multiple_of(ix * TC + (iz + b) % Z * OB, OB), OB), :]
        take(trecv, tr)
        rp4[0] = 10.0 / jnp.sum(trecv[...], axis=0)
        for a in range(1, X):
            send(rp4.at[0], rp4.at[a], ps, pr.at[a], (a, 0, 0, 0))

        col_pass(0)
        col_send(1)
        take(precv, p_r)
        for i in range(BC):
            rows = slice(i * 128, (i + 1) * 128)
            rp = spread(rp4[0, pl.ds(ic * BC + i, 1), :])
            pown[rows, :] = (P1[ic, rows, :] + precv[rows, :]) * jnp.concatenate([rp, rp], axis=1)
        scores_t(0)
        for half, a in enumerate(NEAR):
            take(zall.at[a, ic], xr.at[a])
            relay(a, half)
        for a in NEAR:
            forward(a)
        col_take(1)
        row_send(1)
        for a in NEAR:
            take(rp4.at[a], pr.at[a])
            take(zall.at[a, 1 - ic], fr.at[a])
            scores_t(a)

        col_pass(1)
        col_send(2)
        take(zall.at[FAR, ic], xr.at[FAR])
        forward(FAR)
        take(rp4.at[FAR], pr.at[FAR])
        take(zall.at[FAR, 1 - ic], fr.at[FAR])
        scores_t(FAR)
        col_take(2)
        row_pass(rsend3, range(C))
        for o in sorted(XYC, key=lambda o: o[0] != 0):
            send(rsend3, rrecv3.at[o[0] * GR + YCI[(0,) + o[1:]]], rs.at[4], rr.at[5 if o[0] else 4], o)
        pltpu.make_async_copy(rsend3, rrecv3.at[0], rr.at[4]).start()
        def codes(h):
            for q in range(2):
                rows = pl.ds(pl.multiple_of(h * B + q * HB, HB), HB)
                w = [(K[rows, j * 128 : (j + 1) * 128] * crow[j : j + 1, :]).astype(BF16) for j in range(CC)]
                U[h, q] = dot(jnp.concatenate(w, axis=1), chat[...])

        codes(1 - ic)
        send(U.at[1 - ic], urecv, ks, kr, (0, 0, 1, 0))
        codes(ic)
        mine = crow[pl.ds(ix * (TC // 128), TC // 128), :]
        for i in range(TC // 128):
            c3a[i * 128 : (i + 1) * 128, :] = spread(mine[i : i + 1, :])
        for k, b in enumerate(FZ):
            c3b[k * OB : (k + 1) * OB, :] = c3a[pl.ds(pl.multiple_of((iz + b) % Z * OB, OB), OB), :]
        take(urecv, kr)
        U[ic] = U[ic] + urecv[...]
        take(rrecv3.at[pl.ds(0, GR)], rr.at[4])
        r34[0] = 10.0 / jnp.sum(rrecv3[0:GR], axis=0).reshape(RC, 128)
        for i in range(BC):
            q, rows = i * 128 // HB, slice(i * 128 % HB, i * 128 % HB + 128)
            r3 = spread(r34[0, pl.ds(ic * BC + i, 1), :])
            mine = pown[(1 - q) * HB + i * 128 % HB : (1 - q) * HB + i * 128 % HB + 128, :]
            gpart[1 - q, rows, :] = mine - U[ic, q, rows, :] * jnp.concatenate([r3, r3], axis=1)
        far_y = sorted(range(1, Y), key=lambda k: -ring(k, Y))
        for q in range(2):
            ysend[q] = gpart[q].reshape(Y, HB // Y, D).astype(BF16)
            for f in far_y:
                send(ysend.at[q, (iy + f) % Y], yrecv.at[q, f - 1], ys.at[q], yr.at[q], (0, 0, 0, f))

        def codes_t(rows, sources):
            g = []
            for n in range(sources[0] * RC, (sources[-1] + 1) * RC):
                a, q = n // RC, n % RC
                qp = q // BC * BC + (q + BC // 2) % BC
                g.append(KT[rows, n * 128 : (n + 1) * 128] * r34[a, qp : qp + 1, :].astype(BF16))
            zb = zall[sources[0] : sources[-1] + 1].reshape(len(sources) * RT, D)
            return dot(jnp.concatenate(g, axis=1), zb)

        tpart[...] = codes_t(slice(0, TC), (0,))
        take(rrecv3.at[pl.ds(GR, (X - 1) * GR)], rr.at[5])
        for a in range(1, X):
            r34[a] = 10.0 / jnp.sum(rrecv3[a * GR : (a + 1) * GR], axis=0).reshape(RC, 128)
        parts = 4
        HT, ZH = TC // parts, Z // parts

        def grad_t(m, _):
            rows = pl.ds(pl.multiple_of(m * HT, HT), HT)
            part = tpart[rows, :] + codes_t(rows, range(1, X))
            c3 = c3b[rows, :]
            part = TP[rows, :] - part * jnp.concatenate([c3, c3], axis=1)
            tpart[rows, :] = part
            zsend[pl.ds(m * ZH, ZH)] = part.reshape(ZH, OB, D).astype(BF16)
            for k in range(ZH):
                b = Z // 2 + m * (ZH // 2) + k // 2 if k % 2 == 0 else Z // 2 - m * (ZH // 2) - (k + 1) // 2
                to = {"dp": (ix * Z + (iz + b) % Z) * C + ic, "proto": iy}

                def go(k=k, to=to):
                    pltpu.make_async_remote_copy(
                        src_ref=zsend.at[m * ZH + k], dst_ref=zrecv.at[m * ZH + k], send_sem=zs, recv_sem=zr,
                        device_id=to, device_id_type=MESH,
                    ).start()

                if k < ZH - 1:
                    go()
                else:
                    pl.when(m < parts - 1)(go)
            return 0

        lax.fori_loop(0, parts, grad_t, 0)

        SB = HB // Y
        uc, nc = unit(praw[0, ix * Z + iz].astype(F32))
        units = [unit(ep[pl.ds(pl.multiple_of(q * HB + iy * SB, SB), SB), :].astype(F32)) for q in range(2)]
        for q in range(2):
            uq, nq = units[q]
            take(yrecv.at[q], yr.at[q])
            at = pl.ds(pl.multiple_of(iy * SB, SB), SB)
            gzs = gpart[q, at, :] + jnp.sum(yrecv[q].astype(F32), axis=0)
            yall[q, iy] = ((gzs - uq * jnp.sum(uq * gzs, axis=1, keepdims=True)) / nq).astype(BF16)
            for f in far_y:
                send(yall.at[q, iy], yall.at[q, iy], gs.at[q], gr.at[q], (0, 0, 0, f))

        for q in range(2):
            take(yall.at[q, pl.ds(0, Y - 1)], gr.at[q])
        gz_ref[...] = dot(permt[...], yall[...].reshape(B, D))
        take(zrecv, zr)
        gcs = tpart[(Z - 1) * OB : Z * OB, :] + jnp.sum(zrecv[...].astype(F32), axis=0)
        gc_ref[...] = (gcs - uc * jnp.sum(uc * gcs, axis=1, keepdims=True)) / nc

        take(zall.at[0, ic], core_s)
        take(zall.at[pl.ds(0, X - 1), 0], xs)
        take(zall.at[pl.ds(0, X - 1), 0], fs)
        take(rp4.at[pl.ds(0, X - 1)], ps)
        for t in range(3):
            take(crecv.at[t, pl.ds(0, len(XZ))], cs.at[t])
        take(fsend, f_s)
        take(precv, p_s)
        take(urecv, ks)
        take(trecv.at[pl.ds(0, len(YC))], ts)
        for t in range(2):
            for blk in range(C):
                take(rrecv.at[t, blk, pl.ds(0, len(YC))], rs.at[t * C + blk])
        take(rrecv3.at[pl.ds(0, len(XYC))], rs.at[4])
        take(zrecv, zs)
        for q in range(2):
            take(yrecv.at[q], ys.at[q])
            take(yall.at[q, pl.ds(0, Y - 1)], gs.at[q])

    V = pltpu.VMEM
    S = pltpu.SemaphoreType.DMA
    scratch = [
        V((1, B), jnp.int32),
        V((B, D), BF16),
        V((B, D), BF16),
        V((C, X * Z, OB, D), BF16),
        V((NC, D), BF16),
        V((NC, D), BF16),
        V((B, D), BF16),
        V((B, B), BF16),
        V((B, B), BF16),
        V((X, C, B, D), BF16),
        V((RT, NC), F32),
        V((TC, X * RT), BF16),
        V((C, B, D), F32),
        V((B, D), F32),
        V((B, D), F32),
        V((TC, D), F32),
        V((C, 2, HB, D), F32),
        V((2, HB, D), F32),
        V((8, NC), F32),
        V((RT, 128), F32),
        V((B, 128), F32),
        V((TC, 128), F32),
        V((TC, 128), F32),
        V((TC, D), BF16),
        V((CC, 128), F32),
        V((BC, 128), F32),
        V((X, RC, 128), F32),
        V((X, RC, 128), F32),
        V((3, CC, 128), BF16),
        V((3, len(XZ) + 1, CC, 128), BF16),
        V((CC, 128), F32),
        V((CC, 128), F32),
        V((RC, 128), F32),
        V((GR, RC, 128), F32),
        V((2, C, BC, 128), F32),
        V((2, C, GR, BC, 128), F32),
        V((C, BC, 128), F32),
        V((X * GR, C, BC, 128), F32),
        V((2, HB, D), F32),
        V((TC, D), F32),
        V((Z, OB, D), BF16),
        V((Z - 1, OB, D), BF16),
        V((2, Y, HB // Y, D), BF16),
        V((2, Y - 1, HB // Y, D), BF16),
        V((2, Y, HB // Y, D), BF16),
        S((4,)),
        S, S,
        S, S((X,)),
        S, S((X,)),
        S((3,)), S((3,)),
        S, S,
        S, S,
        S((5,)), S((6,)),
        S, S((X,)),
        S, S,
        S, S,
        S, S,
        S((2,)), S((2,)),
        S((2,)), S((2,)),
    ]
    return kernel, scratch


def place(gz_ref, gc_ref, gz_out, gc_out, sem):
    step = gz_ref.shape[0] // 4
    copies = [pltpu.make_async_copy(gc_ref, gc_out, sem.at[4])]
    for i in range(4):
        rows = pl.ds(i * step, step)
        copies.append(pltpu.make_async_copy(gz_ref.at[rows], gz_out.at[rows], sem.at[i]))
    for copy in copies:
        copy.start()
    for copy in copies:
        copy.wait()


def body(embeddings, prototypes, pair_index):
    B, D = embeddings.shape
    NCL = prototypes.shape[0]
    NC = NCL // C
    OB = NCL // (X * Z * C)
    kernel, scratch = make_kernel(B, D, NC)
    vm = pl.BlockSpec(memory_space=pltpu.VMEM)
    hbm = pl.BlockSpec(memory_space=pl.ANY)
    shapes = (jax.ShapeDtypeStruct((B, D), F32), jax.ShapeDtypeStruct((OB, D), F32))
    held = (pltpu.VMEM((B, D), F32), pltpu.VMEM((OB, D), F32))
    grads = pl.pallas_call(
        kernel,
        out_shape=held,
        in_specs=[hbm, hbm, hbm],
        out_specs=(vm, vm),
        scratch_shapes=scratch,
        compiler_params=pltpu.CompilerParams(
            collective_id=0, has_side_effects=True, vmem_limit_bytes=60 * 2**20
        ),
        name="swav",
    )(embeddings, prototypes.reshape(X * Z, C, OB, D), pair_index.reshape(1, B))
    return pl.pallas_call(
        place,
        out_shape=shapes,
        in_specs=[vm, vm],
        out_specs=(hbm, hbm),
        scratch_shapes=[pltpu.SemaphoreType.DMA((5,))],
        name="place",
    )(*(pltpu.with_memory_space_constraint(g, pltpu.VMEM) for g in grads))


def solution(mesh):
    return jax.shard_map(
        body,
        mesh=mesh,
        in_specs=(P("dp", None), P("proto", None), P("dp")),
        out_specs=(P("dp", None), P(("proto", "dp"), None)),
        check_vma=False,
    )
```

```python
import jax
import jax.numpy as jnp
from jax import lax
from jax.experimental import pallas as pl
from jax.experimental.pallas import tpu as pltpu
from jax.sharding import PartitionSpec as P

X, Z, C, Y = 4, 8, 2, 4
MESH = pl.DeviceIdType.MESH
F32, BF16 = jnp.float32, jnp.bfloat16
NT = (((1,), (1,)), ((), ()))
NN = (((1,), (0,)), ((), ()))


def ring(k, n):
    return min(k, n - k)


def offsets(axes):
    span = [n if a in axes else 1 for a, n in zip("xzcy", (X, Z, C, Y))]
    out = [
        (a, b, e, f)
        for a in range(span[0])
        for b in range(span[1])
        for e in range(span[2])
        for f in range(span[3])
        if a or b or e or f
    ]
    return sorted(out, key=farthest)


def farthest(t):
    return -(4 * (ring(t[0], X) + ring(t[1], Z) + ring(t[3], Y)) + t[2])


def dot(a, b, dims=NN):
    return lax.dot_general(a, b, dims, preferred_element_type=F32)


def unit(values):
    norm = jnp.sqrt(jnp.sum(values * values, axis=1, keepdims=True) + 1e-06)
    return values / norm, norm


def spread(row):
    return jnp.broadcast_to(row, (128, 128)).T


def make_kernel(B, D, NC):
    RT, RC, CC, TC = C * B, C * B // 128, NC // 128, NC // X
    OB = TC // Z
    BC = B // 128
    HB = B // 2
    FZ = [Z // 2 + k // 2 if k % 2 == 0 else Z // 2 - (k + 1) // 2 for k in range(Z)]
    NEAR, FAR = (1, X - 1), 2
    XZ, YC, XYC = offsets("xz"), offsets("yc"), offsets("xyc")

    GR = len(YC) + 1
    YCI = {o: i + 1 for i, o in enumerate(YC)}
    YCI[(0, 0, 0, 0)] = 0

    def kernel(
        emb_ref, proto_ref, pair_ref, gz_ref, gc_ref,
        pair_v, emb_v, zu, praw, chat, chato, ep, perm, permt, zall, K, KT, P1, precv, pown, TP, U, urecv, colacc, racc, rb, c3a, c3b, mine_c,
        crow, rrow, rp4, r34, csend, crecv, fsend, frecv, tsend, trecv, rsend, rrecv, rsend3, rrecv3,
        gpart, tpart, zsend, zrecv, ysend, yrecv, yall,
        lsem, core_s, core_r, xs, xr, fs, fr, cs, cr, f_s, f_r, ts, tr, rs, rr, ps, pr, p_s, p_r, ks, kr, zs, zr, ys, yr, gs, gr,
    ):
        dp = lax.axis_index("dp")
        iy = lax.axis_index("proto")
        ix, iz, ic = dp // (Z * C), (dp // C) % Z, dp % C

        def dev(o):
            a, b, e, f = o
            nx = (ix + a) % X if a else ix
            nz = (iz + b) % Z if b else iz
            nc = (ic + e) % C if e else ic
            ny = (iy + f) % Y if f else iy
            return {"dp": (nx * Z + nz) * C + nc, "proto": ny}

        def send(src, dst, s, r, o):
            pltpu.make_async_remote_copy(
                src_ref=src, dst_ref=dst, send_sem=s, recv_sem=r, device_id=dev(o), device_id_type=MESH
            ).start()

        def take(ref, sem):
            pltpu.make_async_copy(ref, ref, sem).wait()

        loads = [
            pltpu.make_async_copy(pair_ref, pair_v, lsem.at[0]),
            pltpu.make_async_copy(emb_ref, emb_v, lsem.at[1]),
            pltpu.make_async_copy(proto_ref.at[:, 1 - ic], praw.at[1], lsem.at[2]),
            pltpu.make_async_copy(proto_ref.at[:, ic], praw.at[0], lsem.at[3]),
        ]
        for load in loads:
            load.start()
        barrier = pltpu.get_barrier_semaphore()
        everyone = sorted(sorted(set(XZ + YC + XYC)), key=farthest)
        for o in everyone:
            pl.semaphore_signal(barrier, inc=1, device_id=dev(o), device_id_type=MESH)

        loads[1].wait()
        loads[0].wait()
        v = emb_v[...].astype(F32)
        zu[...] = (v * (1.0 / jnp.sqrt(jnp.sum(v * v, axis=1, keepdims=True) + 1e-06))).astype(BF16)
        NB = 256 // OB

        def norm_c(half, out):
            def step(i, _):
                v = praw[half, pl.ds(i * NB, NB)].reshape(256, D).astype(F32)
                inv = 1.0 / jnp.sqrt(jnp.sum(v * v, axis=1, keepdims=True) + 1e-06)
                out[pl.ds(pl.multiple_of(i * 256, 256), 256), :] = (v * inv).astype(BF16)
                return 0

            lax.fori_loop(0, NC // 256, step, 0, unroll=2)

        def first_totals(prototypes, out):
            zb = zu[...]
            for j in range(NC // 256):
                k = jnp.exp(dot(zb, prototypes[j * 256 : (j + 1) * 256, :], NT) * 20.0)
                colacc[:, j * 256 : (j + 1) * 256] = jnp.sum(k.reshape(B // 8, 8, 256), axis=0)
            for j in range(CC):
                out[j : j + 1, :] = jnp.sum(colacc[:, j * 128 : (j + 1) * 128], axis=0, keepdims=True)

        loads[2].wait()
        norm_c(1, chato)
        first_totals(chato, fsend)
        loads[3].wait()
        norm_c(0, chat)
        pl.semaphore_wait(barrier, len(everyone))
        send(fsend, frecv, f_s, f_r, (0, 0, 1, 0))
        first_totals(chat, crow)

        def reorder():
            pair = pair_v[...]
            lane = lax.broadcasted_iota(jnp.int32, (1, B), 1)
            first = (lane < pair).astype(F32)
            up = (
                lax.broadcasted_iota(jnp.int32, (B, B), 0) < lax.broadcasted_iota(jnp.int32, (B, B), 1)
            ).astype(F32).astype(BF16)
            rank = dot(jnp.broadcast_to(first, (8, B)).astype(BF16), up)[0:1, :]
            slot = jnp.where(first > 0.5, rank, -1.0).astype(jnp.int32)
            top = (lax.broadcasted_iota(jnp.int32, (HB, B), 0) == slot).astype(F32).astype(BF16)
            partner = (lax.broadcasted_iota(jnp.int32, (B, B), 0) == pair).astype(F32).astype(BF16)
            perm[0:HB, :] = top
            perm[HB:B, :] = dot(top, partner).astype(BF16)
            ep[...] = dot(perm[...], emb_v[...]).astype(BF16)
            uz, _ = unit(ep[...].astype(F32))
            zall[0, ic] = uz.astype(BF16)

        def scores(h, js):
            rows = pl.ds(pl.multiple_of(h * B, B), B)
            zb = zall[0, h]
            for j in js:
                cols = slice(j * 256, (j + 1) * 256)
                e = jnp.exp(dot(zb, chat[cols, :], NT) * 10.0)
                K[rows, cols] = e * e
                part = dot(e.astype(BF16), chat[cols, :])
                P1[h] = part if j == 0 else P1[h] + part
                two = e[:, :128] + e[:, 128:]
                racc[rows, :] = two if j == 0 else racc[rows, :] + two

        def col_send(t):
            if t:
                for j in range(CC):
                    crow[j : j + 1, :] = jnp.sum(colacc[:, j * 128 : (j + 1) * 128], axis=0, keepdims=True)
            csend[t] = crow[...].astype(BF16)
            for i, o in enumerate(XZ):
                send(csend.at[t], crecv.at[t, i + 1], cs.at[t], cr.at[t], o)
            pltpu.make_async_copy(csend.at[t], crecv.at[t, 0], cr.at[t]).start()

        def col_take(t):
            take(crecv.at[t], cr.at[t])
            crow[...] = 1.0 / jnp.sum(crecv[t].astype(F32), axis=0)

        def row_pass(out, blocks):
            for i in range(blocks[0] * BC, (blocks[-1] + 1) * BC):
                rows = slice(i * 128, (i + 1) * 128)
                acc = jnp.zeros((128, 128), F32)
                for j in range(CC):
                    acc = acc + K[rows, j * 128 : (j + 1) * 128] * crow[j : j + 1, :]
                out[i // BC, i % BC : i % BC + 1, :] = jnp.sum(acc.T, axis=0, keepdims=True)

        def col_pass(t):
            for blk in range(C):
                take(rrecv.at[t, blk], rr.at[t * C + blk])
                rrow[...] = 1.0 / jnp.sum(rrecv[t, blk], axis=0)
                for i in range(BC):
                    rb[i * 128 : (i + 1) * 128, :] = spread(rrow[i : i + 1, :])

                for jg in range(0, CC, 8):
                    acc = [jnp.zeros((8, 128), F32) for _ in range(8)]
                    for i in range(BC):
                        r = rb[i * 128 : (i + 1) * 128, :]
                        rows = slice(blk * B + i * 128, blk * B + (i + 1) * 128)
                        for j in range(8):
                            p = K[rows, (jg + j) * 128 : (jg + j + 1) * 128] * r
                            acc[j] = acc[j] + jnp.sum(p.reshape(16, 8, 128), axis=0)
                    for j in range(8):
                        cols = slice((jg + j) * 128, (jg + j + 1) * 128)
                        colacc[:, cols] = colacc[:, cols] + acc[j] if blk else acc[j]

        def row_send(t):
            for blk in range(C):
                row_pass(rsend.at[t], (blk,))
                for i, o in enumerate(YC):
                    send(rsend.at[t, blk], rrecv.at[t, blk, i + 1], rs.at[t * C + blk], rr.at[t * C + blk], o)
                pltpu.make_async_copy(rsend.at[t, blk], rrecv.at[t, blk, 0], rr.at[t * C + blk]).start()

        def scores_t(a):
            mine = mine_c[...]
            for c in range(C):
                for q in range(B // 256):
                    n = (a * C + c) * (B // 256)
                    zb = zall[a, c, q * 256 : (q + 1) * 256, :]
                    e = jnp.exp(dot(mine, zb, NT) * 10.0)
                    KT[:, (n + 1 - q) * 256 : (n + 2 - q) * 256] = (e * e).astype(BF16)
                    i = c * BC + q * 2
                    p = [
                        (e[:, h * 128 : (h + 1) * 128] * rp4[a, i + h : i + h + 1, :]).astype(BF16) for h in range(2)
                    ]
                    part = dot(jnp.concatenate(p, axis=1), zb)
                    TP[...] = part if a + c + q == 0 else TP[...] + part

        def send_x(a):
            send(zall.at[0, ic], zall.at[a, ic], xs, xr.at[a], (a, 0, 0, 0))

        def forward(a):
            send(zall.at[a, ic], zall.at[a, ic], fs, fr.at[a], (0, 0, 1, 0))

        def relay(a, half):
            rows = pl.ds(half * HB, HB)
            send(zall.at[a, ic, rows], zall.at[FAR, ic, rows], xs, xr.at[FAR], (a, 0, 0, 0))

        take(frecv, f_r)
        crow[...] = crow[...] + frecv[...]
        col_send(0)
        reorder()
        send(zall.at[0, ic], zall.at[0, ic], core_s, core_r, (0, 0, 1, 0))
        for a in NEAR:
            send_x(a)
        scores(ic, range(NC // 256))
        take(zall.at[0, 1 - ic], core_r)
        scores(1 - ic, range(NC // 256))
        send(P1.at[1 - ic], precv, p_s, p_r, (0, 0, 1, 0))
        for i in range(RC):
            tsend[i : i + 1, :] = jnp.sum(racc[i * 128 : (i + 1) * 128, :].T, axis=0, keepdims=True)
        for i, o in enumerate(YC):
            send(tsend, trecv.at[i + 1], ts, tr, o)
        pltpu.make_async_copy(tsend, trecv.at[0], tr).start()
        col_take(0)
        row_send(0)
        permt[...] = perm[...].astype(F32).T.astype(BF16)
        for k, b in enumerate(FZ):
            mine_c[k * OB : (k + 1) * OB, :] = chat[pl.ds(pl.multiple_of(ix * TC + (iz + b) % Z * OB, OB), OB), :]
        take(trecv, tr)
        rp4[0] = 10.0 / jnp.sum(trecv[...], axis=0)
        for a in range(1, X):
            send(rp4.at[0], rp4.at[a], ps, pr.at[a], (a, 0, 0, 0))

        col_pass(0)
        col_send(1)
        take(precv, p_r)
        for i in range(BC):
            rows = slice(i * 128, (i + 1) * 128)
            rp = spread(rp4[0, pl.ds(ic * BC + i, 1), :])
            pown[rows, :] = (P1[ic, rows, :] + precv[rows, :]) * jnp.concatenate([rp, rp], axis=1)
        scores_t(0)
        for half, a in enumerate(NEAR):
            take(zall.at[a, ic], xr.at[a])
            relay(a, half)
        for a in NEAR:
            forward(a)
        col_take(1)
        row_send(1)
        for a in NEAR:
            take(rp4.at[a], pr.at[a])
            take(zall.at[a, 1 - ic], fr.at[a])
            scores_t(a)

        col_pass(1)
        col_send(2)
        take(zall.at[FAR, ic], xr.at[FAR])
        forward(FAR)
        take(rp4.at[FAR], pr.at[FAR])
        take(zall.at[FAR, 1 - ic], fr.at[FAR])
        scores_t(FAR)
        col_take(2)
        row_pass(rsend3, range(C))
        for o in sorted(XYC, key=lambda o: o[0] != 0):
            send(rsend3, rrecv3.at[o[0] * GR + YCI[(0,) + o[1:]]], rs.at[4], rr.at[5 if o[0] else 4], o)
        pltpu.make_async_copy(rsend3, rrecv3.at[0], rr.at[4]).start()
        def codes(h, other):
            for q in range(2):
                rows = pl.ds(pl.multiple_of(h * B + q * HB, HB), HB)
                w = [(K[rows, j * 128 : (j + 1) * 128] * crow[j : j + 1, :]).astype(BF16) for j in range(CC)]
                U[h, q] = dot(jnp.concatenate(w, axis=1), chat[...])
                if other:
                    send(U.at[h, q], urecv.at[q], ks.at[q], kr.at[q], (0, 0, 1, 0))

        codes(1 - ic, True)
        codes(ic, False)
        mine = crow[pl.ds(ix * (TC // 128), TC // 128), :]
        for i in range(TC // 128):
            c3a[i * 128 : (i + 1) * 128, :] = spread(mine[i : i + 1, :])
        for k, b in enumerate(FZ):
            c3b[k * OB : (k + 1) * OB, :] = c3a[pl.ds(pl.multiple_of((iz + b) % Z * OB, OB), OB), :]
        for q in range(2):
            take(urecv.at[q], kr.at[q])
            U[ic, q] = U[ic, q] + urecv[q]
        take(rrecv3.at[pl.ds(0, GR)], rr.at[4])
        r34[0] = 10.0 / jnp.sum(rrecv3[0:GR], axis=0).reshape(RC, 128)
        for i in range(BC):
            q, rows = i * 128 // HB, slice(i * 128 % HB, i * 128 % HB + 128)
            r3 = spread(r34[0, pl.ds(ic * BC + i, 1), :])
            mine = pown[(1 - q) * HB + i * 128 % HB : (1 - q) * HB + i * 128 % HB + 128, :]
            gpart[1 - q, rows, :] = mine - U[ic, q, rows, :] * jnp.concatenate([r3, r3], axis=1)
        far_y = sorted(range(1, Y), key=lambda k: -ring(k, Y))
        for q in range(2):
            ysend[q] = gpart[q].reshape(Y, HB // Y, D).astype(BF16)
            for f in far_y:
                send(ysend.at[q, (iy + f) % Y], yrecv.at[q, f - 1], ys.at[q], yr.at[q], (0, 0, 0, f))

        def codes_t(rows, sources):
            g = []
            for n in range(sources[0] * RC, (sources[-1] + 1) * RC):
                a, q = n // RC, n % RC
                qp = q // BC * BC + (q + BC // 2) % BC
                g.append(KT[rows, n * 128 : (n + 1) * 128] * r34[a, qp : qp + 1, :].astype(BF16))
            zb = zall[sources[0] : sources[-1] + 1].reshape(len(sources) * RT, D)
            return dot(jnp.concatenate(g, axis=1), zb)

        tpart[...] = codes_t(slice(0, TC), (0,))
        take(rrecv3.at[pl.ds(GR, (X - 1) * GR)], rr.at[5])
        for a in range(1, X):
            r34[a] = 10.0 / jnp.sum(rrecv3[a * GR : (a + 1) * GR], axis=0).reshape(RC, 128)
        parts = 4
        HT, ZH = TC // parts, Z // parts

        def grad_t(m, _):
            rows = pl.ds(pl.multiple_of(m * HT, HT), HT)
            part = tpart[rows, :] + codes_t(rows, range(1, X))
            c3 = c3b[rows, :]
            part = TP[rows, :] - part * jnp.concatenate([c3, c3], axis=1)
            tpart[rows, :] = part
            zsend[pl.ds(m * ZH, ZH)] = part.reshape(ZH, OB, D).astype(BF16)
            for k in range(ZH):
                b = Z // 2 + m * (ZH // 2) + k // 2 if k % 2 == 0 else Z // 2 - m * (ZH // 2) - (k + 1) // 2
                to = {"dp": (ix * Z + (iz + b) % Z) * C + ic, "proto": iy}

                def go(k=k, to=to):
                    pltpu.make_async_remote_copy(
                        src_ref=zsend.at[m * ZH + k], dst_ref=zrecv.at[m * ZH + k], send_sem=zs, recv_sem=zr,
                        device_id=to, device_id_type=MESH,
                    ).start()

                if k < ZH - 1:
                    go()
                else:
                    pl.when(m < parts - 1)(go)
            return 0

        lax.fori_loop(0, parts, grad_t, 0)

        SB = HB // Y
        uc, nc = unit(praw[0, ix * Z + iz].astype(F32))
        units = [unit(ep[pl.ds(pl.multiple_of(q * HB + iy * SB, SB), SB), :].astype(F32)) for q in range(2)]
        for q in range(2):
            uq, nq = units[q]
            take(yrecv.at[q], yr.at[q])
            at = pl.ds(pl.multiple_of(iy * SB, SB), SB)
            gzs = gpart[q, at, :] + jnp.sum(yrecv[q].astype(F32), axis=0)
            yall[q, iy] = ((gzs - uq * jnp.sum(uq * gzs, axis=1, keepdims=True)) / nq).astype(BF16)
            for f in far_y:
                send(yall.at[q, iy], yall.at[q, iy], gs.at[q], gr.at[q], (0, 0, 0, f))

        for q in range(2):
            take(yall.at[q, pl.ds(0, Y - 1)], gr.at[q])
        gz_ref[...] = dot(permt[...], yall[...].reshape(B, D))
        take(zrecv, zr)
        gcs = tpart[(Z - 1) * OB : Z * OB, :] + jnp.sum(zrecv[...].astype(F32), axis=0)
        gc_ref[...] = (gcs - uc * jnp.sum(uc * gcs, axis=1, keepdims=True)) / nc

        take(zall.at[0, ic], core_s)
        take(zall.at[pl.ds(0, X - 1), 0], xs)
        take(zall.at[pl.ds(0, X - 1), 0], fs)
        take(rp4.at[pl.ds(0, X - 1)], ps)
        for t in range(3):
            take(crecv.at[t, pl.ds(0, len(XZ))], cs.at[t])
        take(fsend, f_s)
        take(precv, p_s)
        for q in range(2):
            take(urecv.at[q], ks.at[q])
        take(trecv.at[pl.ds(0, len(YC))], ts)
        for t in range(2):
            for blk in range(C):
                take(rrecv.at[t, blk, pl.ds(0, len(YC))], rs.at[t * C + blk])
        take(rrecv3.at[pl.ds(0, len(XYC))], rs.at[4])
        take(zrecv, zs)
        for q in range(2):
            take(yrecv.at[q], ys.at[q])
            take(yall.at[q, pl.ds(0, Y - 1)], gs.at[q])

    V = pltpu.VMEM
    S = pltpu.SemaphoreType.DMA
    scratch = [
        V((1, B), jnp.int32),
        V((B, D), BF16),
        V((B, D), BF16),
        V((C, X * Z, OB, D), BF16),
        V((NC, D), BF16),
        V((NC, D), BF16),
        V((B, D), BF16),
        V((B, B), BF16),
        V((B, B), BF16),
        V((X, C, B, D), BF16),
        V((RT, NC), F32),
        V((TC, X * RT), BF16),
        V((C, B, D), F32),
        V((B, D), F32),
        V((B, D), F32),
        V((TC, D), F32),
        V((C, 2, HB, D), F32),
        V((2, HB, D), F32),
        V((8, NC), F32),
        V((RT, 128), F32),
        V((B, 128), F32),
        V((TC, 128), F32),
        V((TC, 128), F32),
        V((TC, D), BF16),
        V((CC, 128), F32),
        V((BC, 128), F32),
        V((X, RC, 128), F32),
        V((X, RC, 128), F32),
        V((3, CC, 128), BF16),
        V((3, len(XZ) + 1, CC, 128), BF16),
        V((CC, 128), F32),
        V((CC, 128), F32),
        V((RC, 128), F32),
        V((GR, RC, 128), F32),
        V((2, C, BC, 128), F32),
        V((2, C, GR, BC, 128), F32),
        V((C, BC, 128), F32),
        V((X * GR, C, BC, 128), F32),
        V((2, HB, D), F32),
        V((TC, D), F32),
        V((Z, OB, D), BF16),
        V((Z - 1, OB, D), BF16),
        V((2, Y, HB // Y, D), BF16),
        V((2, Y - 1, HB // Y, D), BF16),
        V((2, Y, HB // Y, D), BF16),
        S((4,)),
        S, S,
        S, S((X,)),
        S, S((X,)),
        S((3,)), S((3,)),
        S, S,
        S, S,
        S((5,)), S((6,)),
        S, S((X,)),
        S, S,
        S((2,)), S((2,)),
        S, S,
        S((2,)), S((2,)),
        S((2,)), S((2,)),
    ]
    return kernel, scratch


def place(gz_ref, gc_ref, gz_out, gc_out, sem):
    step = gz_ref.shape[0] // 4
    copies = [pltpu.make_async_copy(gc_ref, gc_out, sem.at[4])]
    for i in range(4):
        rows = pl.ds(i * step, step)
        copies.append(pltpu.make_async_copy(gz_ref.at[rows], gz_out.at[rows], sem.at[i]))
    for copy in copies:
        copy.start()
    for copy in copies:
        copy.wait()


def body(embeddings, prototypes, pair_index):
    B, D = embeddings.shape
    NCL = prototypes.shape[0]
    NC = NCL // C
    OB = NCL // (X * Z * C)
    kernel, scratch = make_kernel(B, D, NC)
    vm = pl.BlockSpec(memory_space=pltpu.VMEM)
    hbm = pl.BlockSpec(memory_space=pl.ANY)
    shapes = (jax.ShapeDtypeStruct((B, D), F32), jax.ShapeDtypeStruct((OB, D), F32))
    held = (pltpu.VMEM((B, D), F32), pltpu.VMEM((OB, D), F32))
    grads = pl.pallas_call(
        kernel,
        out_shape=held,
        in_specs=[hbm, hbm, hbm],
        out_specs=(vm, vm),
        scratch_shapes=scratch,
        compiler_params=pltpu.CompilerParams(
            collective_id=0, has_side_effects=True, vmem_limit_bytes=60 * 2**20
        ),
        name="swav",
    )(embeddings, prototypes.reshape(X * Z, C, OB, D), pair_index.reshape(1, B))
    return pl.pallas_call(
        place,
        out_shape=shapes,
        in_specs=[vm, vm],
        out_specs=(hbm, hbm),
        scratch_shapes=[pltpu.SemaphoreType.DMA((5,))],
        name="place",
    )(*(pltpu.with_memory_space_constraint(g, pltpu.VMEM) for g in grads))


def solution(mesh):
    return jax.shard_map(
        body,
        mesh=mesh,
        in_specs=(P("dp", None), P("proto", None), P("dp")),
        out_specs=(P("dp", None), P(("proto", "dp"), None)),
        check_vma=False,
    )
```
